128 devices in a mesh: dp: 32 (over y, z, core), group: 4 (over x).
Axes of the slice: x: 4, y: 4, z: 4, core: 2. Of those that a mesh axis runs over, the one named last changes fastest.
Arguments:
- token_tiles: bfloat16 [32, 4, 64, 128, 128], P('dp', 'group'), may hold values from -6 to 6
- segment_ids: int32 [32, 4, 64, 128], P('dp', 'group'), may hold values from -1 to 34, as said below
- visible_flags: int32 [32, 4, 64, 128], P('dp', 'group'), may hold values 0 or 1
- tile_order: int32 [32, 4, 64], P('dp', 'group'), may hold values from 0 to 63, each once within a row
- mask_token: float32 [128], replicated, may hold values from -4 to 4
- norm_gains: float32 [2, 2, 128], replicated, may hold values from 0.25 to 1.75
- shift_terms: float32 [2, 4, 128], replicated, may hold values from -2 to 2
- attn_in: bfloat16 [2, 128, 384], replicated, may hold values from -0.5 to 0.5
- attn_out: bfloat16 [2, 128, 128], replicated, may hold values from -1.5 to 1.5
- mlp_in: bfloat16 [2, 128, 512], replicated, may hold values from -0.5 to 0.5
- hidden_shift: float32 [2, 512], replicated, may hold values from -2 to 2
- mlp_out: bfloat16 [2, 512, 128], replicated, may hold values from -0.25 to 0.25
- cotangent: bfloat16 [32, 4, 64, 128, 128], P('dp', 'group'), may hold values from -6 to 6
Outputs:
- decoded: bfloat16 [32, 4, 64, 128, 128], P('dp', 'group')
- tiles_grad: float32 [32, 4, 64, 128, 128], P('dp', 'group')
- mask_grad: float32 [128], replicated
- gains_grad: float32 [2, 2, 128], replicated
- shifts_grad: float32 [2, 4, 128], replicated
- attn_in_grad: float32 [2, 128, 384], replicated
- attn_out_grad: float32 [2, 128, 128], replicated
- mlp_in_grad: float32 [2, 128, 512], replicated
- hidden_grad: float32 [2, 512], replicated
- mlp_out_grad: float32 [2, 512, 128], replicated
The draws below stay inside these ranges and needn't reach their ends.
Inputs may be any that keep to these rules, and one draw needn't show every extreme that they name: `segment_ids`: in each tile the slots of a series hold one id; series are numbered 0, 1, 2, ... from the tile's start, each of 3 to 24 slots, one of exactly 24 in every tile; slots after the last series are padding with id -1. `tile_order`: for every device, a permutation of the numbers of its 64 tiles.
All inputs are finite; a program needn't handle non-finite values. No bound on the sum of `visible_flags` on one device may be relied on, other than what follows from the above.
Results may differ from the reference program's by a relative error of at most 0.017.
Values may be sent and summed in bfloat16 or wider, within the bound.
No kernel may reach another device: no remote copies, remote signals or barrier semaphores. Data moves between devices by JAX's collectives and lax.ppermute only.
A program may use at most 256 MiB of HBM per device.

```python
import math
import jax
import jax.numpy as jnp
from jax import lax

D = 128
HEADS = 8
HEAD = 16
FF = 512
SLOTS = 128
SERIES = 24
TILES_DEV = 64
N_DP = 32
N_GROUP = 4


def draw_segment_ids(key, part):
    key = jax.random.fold_in(key, 11)
    series_count = SLOTS // 3 + 2
    lengths = jax.random.randint(key, (N_DP, N_GROUP, TILES_DEV, series_count), 3, SERIES + 1)
    first_tile = (jnp.arange(TILES_DEV, dtype=jnp.int32) == 0)[None, None, :, None]
    lengths = jnp.where(first_tile, 3, lengths)
    lengths = lengths.at[..., 1].set(SERIES)
    bounds = jnp.cumsum(lengths, axis=-1)
    positions = jnp.arange(SLOTS, dtype=jnp.int32)
    numbers = jnp.sum((bounds[..., None, :] <= positions[:, None]).astype(jnp.int32), axis=-1)
    finish = jnp.take_along_axis(bounds, jnp.minimum(numbers, series_count - 1), axis=-1)
    return jnp.where(finish <= SLOTS, numbers, -1).astype(jnp.int32)


def touch_ends(array, stream_key, smallest, high):
    longest = array.shape.index(max(array.shape))
    spots = []
    for shift in (0, 1):
        where = [jax.random.randint(jax.random.fold_in(stream_key, axis), (), 0, length) for axis, length in enumerate(array.shape)]
        where[longest] = (where[longest] + shift) % array.shape[longest]
        spots.append(tuple(where))
    return array.at[spots[0]].set(smallest).at[spots[1]].set(high)


def block_scale(stream_key, extent, split, least, top_value):
    factor_of = 1.0
    for axis_at, blocks in split:
        steps = jax.random.uniform(jax.random.fold_in(jax.random.fold_in(stream_key, 6), axis_at), (blocks,), jnp.float32, least / len(split), top_value / len(split))
        factor_of = factor_of * jnp.repeat(jnp.exp(steps), extent[axis_at] // blocks).reshape((-1,) + (1,) * (len(extent) - 1 - axis_at))
    return factor_of


def gaussian(own_key, dims, deviation, reach, split=(), kind=jnp.bfloat16):
    drawn = deviation * jax.random.normal(own_key, dims, jnp.float32)
    if split:
        drawn = drawn * block_scale(own_key, dims, split, -0.22, 0.18)
    return jnp.clip(drawn, -reach, reach).astype(kind)


def setup_inputs(seed: int = 0) -> dict:
    key_of = jax.random.split(jax.random.key(seed), 14)
    return {
        "token_tiles": gaussian(key_of[0], (N_DP, N_GROUP, TILES_DEV, SLOTS, D), 1.0, 6.0, ((0, 32), (1, 4))),
        "segment_ids": draw_segment_ids(jax.random.fold_in(key_of[13], 71), 0),
        "visible_flags": touch_ends((jax.random.randint(key_of[2], (N_DP, N_GROUP, TILES_DEV, SLOTS), 0, 5) < 3).astype(jnp.int32), jax.random.fold_in(key_of[2], 1), 0, 1),
        "tile_order": jax.vmap(lambda own: jax.random.permutation(own, TILES_DEV))(jax.random.split(key_of[3], N_DP * N_GROUP)).reshape((N_DP, N_GROUP, TILES_DEV)).astype(jnp.int32),
        "mask_token": gaussian(key_of[4], (D,), 1.0, 4.0, (), jnp.float32),
        "norm_gains": jnp.clip(1.0 + 0.15 * jax.random.normal(key_of[5], (2, 2, D), jnp.float32), 0.25, 1.75),
        "shift_terms": gaussian(key_of[6], (2, 4, D), 0.3, 2.0, (), jnp.float32),
        "attn_in": gaussian(key_of[7], (2, D, 3 * D), D ** -0.5, 0.5),
        "attn_out": gaussian(key_of[8], (2, D, D), (D // 8) ** -0.5, 1.5),
        "mlp_in": gaussian(key_of[9], (2, D, FF), D ** -0.5, 0.5),
        "hidden_shift": gaussian(key_of[10], (2, FF), 0.3, 2.0, (), jnp.float32),
        "mlp_out": gaussian(key_of[11], (2, FF, D), FF ** -0.5, 0.25),
        "cotangent": gaussian(key_of[12], (N_DP, N_GROUP, TILES_DEV, SLOTS, D), 1.0, 6.0, ((0, 32), (1, 4))),
    }


epsilon = 1e-05
highest = lax.Precision.HIGHEST

@jax.custom_vjp
def low(v):
    return lax.optimization_barrier(v.astype(jnp.bfloat16)).astype(jnp.float32)

@jax.custom_vjp
def low_back(v):
    return v

def low_keep(v):
    return (low(v), None)

def low_pass(kept, grad):
    return (grad,)

def back_keep(v):
    return (v, None)

def back_low(kept, grad):
    return (low(grad),)
low.defvjp(low_keep, low_pass)
low_back.defvjp(back_keep, back_low)

def layer_norm(values, gain_row, shift_row):
    center = values - lax.optimization_barrier(jnp.mean(values, axis=-1, keepdims=True))
    spread = lax.optimization_barrier(jnp.mean(center * center, axis=-1, keepdims=True))
    return center * lax.rsqrt(spread + epsilon) * gain_row + shift_row

def gelu_exact(values):
    return 0.5 * values * (1.0 + lax.erf(values * 0.7071067811865476))

def allowed_mask(segments, flag_rows, decoder):
    same_series = (segments[:, :, None] == segments[:, None, :]) & (segments[:, :, None] >= 0)
    if not decoder:
        same_series = same_series & (flag_rows[:, None, :] == 1)
    diagonal = jnp.eye(segments.shape[1], dtype=bool)
    return same_series | diagonal[None]

def run_layer(params, stream, allowed):
    gain_pair, shift_four, attn_in, attn_out, mlp_in, hidden_shift, mlp_out = params
    tile_count, slot_count, model_width = stream.shape
    normed = low(layer_norm(stream, gain_pair[0], shift_four[0]))
    packed = low(low_back(jnp.einsum('tsd,de->tse', normed, attn_in, precision=highest)))
    pieces = packed.reshape(tile_count, slot_count, 3, HEADS, HEAD)
    scores = jnp.einsum('bqhc,bkhc->bhqk', pieces[:, :, 0], pieces[:, :, 1], precision=highest) * HEAD ** (-0.5)
    scores = low_back(jnp.where(allowed[:, None], scores, -1e+30))
    weights = low(jax.nn.softmax(scores, axis=-1))
    mixture = jnp.einsum('bhqk,bkhc->bqhc', weights, pieces[:, :, 2], precision=highest)
    mixture = low(low_back(mixture.reshape(tile_count, slot_count, model_width)))
    branch = low_back(jnp.einsum('tsd,de->tse', mixture, attn_out, precision=highest) + shift_four[2])
    middle = stream + branch
    second = low(layer_norm(middle, gain_pair[1], shift_four[1]))
    hidden = low_back(jnp.einsum('tsd,df->tsf', second, mlp_in, precision=highest) + hidden_shift)
    active = low(gelu_exact(hidden))
    return middle + low_back(jnp.einsum('tsf,fd->tsd', active, mlp_out, precision=highest) + shift_four[3])

def run_blocks(stream, segments, flag_rows, params, decoder):
    full_shape = stream.shape
    slot_count = full_shape[-2]
    flattened = stream.reshape((-1,) + full_shape[-2:])
    tile_count = flattened.shape[0]
    group_size = math.gcd(tile_count, max(1, 4096 // slot_count))
    blocks = tile_count // group_size

    def block_layer(layer_params, inputs):
        stream_blk, seg_blk, flag_blk = inputs
        return run_layer(layer_params, stream_blk, allowed_mask(seg_blk, flag_blk, decoder))
    saved_layer = jax.checkpoint(block_layer)

    def one_block(inputs):
        return saved_layer(params, inputs)
    result = lax.map(one_block, (flattened.reshape((blocks, group_size) + full_shape[-2:]), segments.reshape(blocks, group_size, slot_count), flag_rows.reshape(blocks, group_size, slot_count)))
    return result.reshape(full_shape)

def relayout(array_in, tile_order):
    index_rows = tile_order.reshape(tile_order.shape + (1,) * (array_in.ndim - 3)).astype(jnp.int32)
    ordered = jnp.take_along_axis(array_in, index_rows, axis=2)
    per_peer = array_in.shape[2] // N_DP
    split_up = ordered.reshape((N_DP, N_GROUP, N_DP, per_peer) + array_in.shape[3:])
    return jnp.swapaxes(split_up, 0, 2).reshape(array_in.shape)

def forward(tiles_f, mask_f, gains_f, shifts_f, attn_in_f, attn_out_f, mlp_in_f, hidden_f, mlp_out_f, segment_ids, visible_flags, tile_order):
    encoder_params = (gains_f[0], shifts_f[0], attn_in_f[0], attn_out_f[0], mlp_in_f[0], hidden_f[0], mlp_out_f[0])
    decoder_params = (gains_f[1], shifts_f[1], attn_in_f[1], attn_out_f[1], mlp_in_f[1], hidden_f[1], mlp_out_f[1])
    encoded = run_blocks(tiles_f, segment_ids, visible_flags, encoder_params, False)
    encoded = low(low_back(encoded))
    relaid = relayout(encoded, tile_order)
    relaid_seg = relayout(segment_ids, tile_order)
    relaid_vis = relayout(visible_flags, tile_order)
    decoder_in = jnp.where(relaid_vis[..., None] == 1, relaid, mask_f)
    return run_blocks(decoder_in, relaid_seg, relaid_vis, decoder_params, True)

def reference(token_tiles, segment_ids, visible_flags, tile_order, mask_token, norm_gains, shift_terms, attn_in, attn_out, mlp_in, hidden_shift, mlp_out, cotangent):

    def wrapped(tiles_f, mask_f, gains_f, shifts_f, attn_in_f, attn_out_f, mlp_in_f, hidden_f, mlp_out_f):
        return forward(tiles_f, mask_f, gains_f, shifts_f, attn_in_f, attn_out_f, mlp_in_f, hidden_f, mlp_out_f, segment_ids, visible_flags, tile_order)
    primals = (token_tiles.astype(jnp.float32), mask_token.astype(jnp.float32), norm_gains.astype(jnp.float32), shift_terms.astype(jnp.float32), attn_in.astype(jnp.float32), attn_out.astype(jnp.float32), mlp_in.astype(jnp.float32), hidden_shift.astype(jnp.float32), mlp_out.astype(jnp.float32))
    decoded, pull_back = jax.vjp(wrapped, *primals)
    gradients = pull_back(cotangent.astype(jnp.float32))
    return (decoded.astype(jnp.bfloat16), gradients[0], gradients[1], gradients[2], gradients[3], gradients[4], gradients[5], gradients[6], gradients[7], gradients[8])
```

```python
import jax
import jax.numpy as jnp
from jax import lax
from jax.experimental import pallas as pl
from jax.experimental.pallas import tpu as pltpu
from jax.sharding import PartitionSpec as P

HEADS = 8
HEAD = 16
D = 128
FF = 512
S = 128
NT = 2
L = NT * S
EPS = 1e-5
LOG2E = 1.4426950408889634
LN2 = 0.6931471805599453
F32 = jnp.float32
BF = jnp.bfloat16


def nn(a, b):
    return lax.dot_general(a, b, (((1,), (0,)), ((), ())), preferred_element_type=F32)


def nt(a, b):
    return lax.dot_general(a, b, (((1,), (1,)), ((), ())), preferred_element_type=F32)


def wide(col):
    return jnp.concatenate([col] * NT, axis=1)


def fold(val):
    out = val[:, :S]
    for t in range(1, NT):
        out = out + val[:, t * S:(t + 1) * S]
    return out


def normalize(x):
    center = x - jnp.sum(x, axis=0, keepdims=True) * (1.0 / D)
    var = jnp.sum(center * center, axis=0, keepdims=True) * (1.0 / D)
    rstd = lax.rsqrt(var + EPS)
    return center * rstd, rstd


def norm_back(grad, xhat, rstd, gain):
    gx = grad * gain
    m1 = jnp.sum(gx, axis=0, keepdims=True) * (1.0 / D)
    m2 = jnp.sum(gx * xhat, axis=0, keepdims=True) * (1.0 / D)
    return (gx - m1 - xhat * m2) * rstd


def padded(rows, h):
    parts = []
    if h > 0:
        parts.append(jnp.zeros((HEAD * h, S), BF))
    parts.append(rows)
    if h < HEADS - 1:
        parts.append(jnp.zeros((D - HEAD * (h + 1), S), BF))
    return jnp.concatenate(parts, axis=0)


def layer_fwd(l, x, biases, w, scr):
    cols, hid, wi_t, wi, wo_t, wo, m1_t, m1, m2_t, m2 = w
    e_ref, p_ref, inv_ref, o_ref, u_ref, gp_ref = scr
    xhat0, rstd0 = normalize(x)
    a = (xhat0 * wide(cols[l, 0]) + wide(cols[l, 2])).astype(BF)
    p = nn(wi_t[l], a)
    p_ref[l, 0:D, :] = (p[0:D] * (0.25 * LOG2E)).astype(BF)
    p_ref[l, D:3 * D, :] = p[D:3 * D].astype(BF)
    ones = jnp.ones((HEAD, S), BF)
    for t in range(NT):
        sl = slice(t * S, (t + 1) * S)
        keys = jnp.transpose(p_ref[l, D:2 * D, sl])
        for h in range(HEADS):
            hs = slice(HEAD * h, HEAD * (h + 1))
            s = nn(keys, padded(p_ref[l, hs, sl], h)) + biases[t]
            e = jnp.exp2(s - jnp.max(s, axis=0, keepdims=True)).astype(BF)
            e_ref[l, t, h] = e
            v = p_ref[l, 2 * D + HEAD * h:2 * D + HEAD * (h + 1), sl]
            o = nn(jnp.concatenate([v, ones], axis=0), e)
            inv = 1.0 / o[HEAD:HEAD + 8]
            inv_ref[l, 8 * h:8 * h + 8, sl] = inv
            o_ref[l, hs, sl] = o[0:HEAD] * jnp.concatenate([inv, inv], axis=0)
    ob = o_ref[l].astype(BF)
    x1 = x + nn(wo_t[l], ob) + wide(cols[l, 4])
    xhat1, rstd1 = normalize(x1)
    b = (xhat1 * wide(cols[l, 1]) + wide(cols[l, 3])).astype(BF)
    hidden = nn(m1_t[l], b) + wide(hid[l])
    cdf = 0.5 * lax.erf(hidden * 0.7071067811865476) + 0.5
    u = (hidden * cdf).astype(BF)
    u_ref[l] = u
    phi = jnp.exp2(hidden * hidden * (-0.5 * LOG2E)) * 0.3989422804014327
    gp_ref[l] = (cdf + hidden * phi).astype(BF)
    x2 = x1 + nn(m2_t[l], u) + wide(cols[l, 5])
    return x2, (xhat0, rstd0, a, ob, xhat1, rstd1, b)


def layer_bwd(l, g2, saved, w, scr, acc):
    cols, hid, wi_t, wi, wo_t, wo, m1_t, m1, m2_t, m2 = w
    e_ref, p_ref, inv_ref, o_ref, u_ref, gp_ref = scr
    a_vec, a_hid, a_wi, a_wo, a_m1, a_m2 = acc
    xhat0, rstd0, a, ob, xhat1, rstd1, b = saved
    gz = g2.astype(BF)
    a_vec[l, 5] += fold(g2)
    a_m2[l] += nt(u_ref[l], gz)
    gh = nn(m2[l], gz) * gp_ref[l].astype(F32)
    a_hid[l] += fold(gh)
    ghb = gh.astype(BF)
    a_m1[l] += nt(ghb, b)
    gb = nn(m1[l], ghb)
    a_vec[l, 1] += fold(gb * xhat1)
    a_vec[l, 3] += fold(gb)
    g1 = g2 + norm_back(gb, xhat1, rstd1, wide(cols[l, 1]))
    gy = g1.astype(BF)
    a_vec[l, 4] += fold(g1)
    a_wo[l] += nt(ob, gy)
    go = nn(wo[l], gy)
    gps = []
    for t in range(NT):
        sl = slice(t * S, (t + 1) * S)
        values = jnp.transpose(p_ref[l, 2 * D:3 * D, sl])
        gq, gk, gv = [], [], []
        for h in range(HEADS):
            hs = slice(HEAD * h, HEAD * (h + 1))
            inv = inv_ref[l, 8 * h:8 * h + 8, sl]
            gob = (go[hs, sl] * jnp.concatenate([inv, inv], axis=0)).astype(BF)
            r = jnp.sum(gob.astype(F32) * o_ref[l, hs, sl], axis=0, keepdims=True)
            e = e_ref[l, t, h]
            gs = (e.astype(F32) * (nn(values, padded(gob, h)) - r)).astype(BF)
            gv.append(nt(gob, e))
            gq.append(nn(p_ref[l, D + HEAD * h:D + HEAD * (h + 1), sl], gs) * 0.25)
            gk.append(nt(p_ref[l, hs, sl], gs) * LN2)
        gps.append(jnp.concatenate(gq + gk + gv, axis=0).astype(BF))
    gp = jnp.concatenate(gps, axis=1)
    a_wi[l] += nt(gp, a)
    ga = nn(wi[l], gp)
    a_vec[l, 0] += fold(ga * xhat0)
    a_vec[l, 2] += fold(ga)
    return g1 + norm_back(ga, xhat0, rstd0, wide(cols[l, 0]))


def kernel(inv_order, x_ref, *rest):
    cots = rest[:NT]
    (seg_ref, vis_ref, cols, hid, maskcol, wi_t, wi, wo_t, wo, m1_t, m1, m2_t, m2,
     dec_ref, tg_ref, o_m2, o_m1, o_wi, o_wo, o_row,
     a_vec, a_mask, a_hid, a_m2, a_m1, a_wi, a_wo,
     e_ref, p_ref, i_ref, o_ref, u_ref, gp_ref) = rest[NT:]
    step = pl.program_id(0)
    acc = (a_vec, a_hid, a_wi, a_wo, a_m1, a_m2)

    @pl.when(step == 0)
    def _():
        for ref in acc + (a_mask,):
            ref[...] = jnp.zeros_like(ref)

    w = (cols, hid, wi_t, wi, wo_t, wo, m1_t, m1, m2_t, m2)
    scr = (e_ref, p_ref, i_ref, o_ref, u_ref, gp_ref)
    rows_i = lax.broadcasted_iota(jnp.int32, (S, S), 0)
    cols_i = lax.broadcasted_iota(jnp.int32, (S, S), 1)
    diag = rows_i == cols_i
    eye = diag.astype(F32).astype(BF)
    bias_e, bias_d = [], []
    for t in range(NT):
        seg = seg_ref[0, t:t + 1, :]
        vis = vis_ref[0, t:t + 1, :]
        code = jnp.where(seg >= 0, seg, -2) * 2 + jnp.where(vis == 1, 1, 0)
        code_k = jnp.transpose(jnp.broadcast_to(code, (S, S)).astype(F32))
        diff = code_k - (2 * seg).astype(F32)
        bias_e.append(jnp.where((diff == 1.0) | diag, 0.0, -1e30))
        bias_d.append(jnp.where((diff == 1.0) | (diff == 0.0) | diag, 0.0, -1e30))
    x = jnp.concatenate([nt(eye, x_ref[t]) for t in range(NT)], axis=1)
    enc, saved_e = layer_fwd(0, x, bias_e, w, scr)
    shown = jnp.concatenate([vis_ref[0, t:t + 1, :] for t in range(NT)], axis=1) == 1
    dec_in = jnp.where(shown, enc.astype(BF).astype(F32), wide(maskcol[...]))
    dec, saved_d = layer_fwd(1, dec_in, bias_d, w, scr)
    decb = dec.astype(BF)
    for t in range(NT):
        dec_ref[t] = nt(eye, decb[:, t * S:(t + 1) * S]).astype(BF)
    g = jnp.concatenate([nt(eye, c[0]) for c in cots], axis=1)
    g = layer_bwd(1, g, saved_d, w, scr, acc)
    a_mask[...] += fold(jnp.where(shown, 0.0, g))
    g = jnp.where(shown, g, 0.0).astype(BF).astype(F32)
    g = layer_bwd(0, g, saved_e, w, scr, acc)
    for t in range(NT):
        tg_ref[t] = jnp.transpose(g[:, t * S:(t + 1) * S])

    @pl.when(step == pl.num_programs(0) - 1)
    def _():
        o_m2[...] = a_m2[...]
        o_wo[...] = a_wo[...]
        for l in range(2):
            o_m1[l] = jnp.transpose(a_m1[l])
            o_wi[l] = jnp.transpose(a_wi[l])
            for j in range(6):
                o_row[6 * l + j:6 * l + j + 1, :] = jnp.sum(jnp.transpose(a_vec[l, j]), axis=0, keepdims=True)
            for j in range(4):
                o_row[12 + 4 * l + j:13 + 4 * l + j, :] = jnp.sum(
                    jnp.transpose(a_hid[l, j * D:(j + 1) * D]), axis=0, keepdims=True)
        o_row[20:21, :] = jnp.sum(jnp.transpose(a_mask[...]), axis=0, keepdims=True)
        o_row[21:24, :] = jnp.zeros((3, D), F32)


def local_compute(x, seg, vis, inv_order, cot, cols, hid, maskcol, weights):
    tiles = x.shape[0]
    steps = tiles // NT
    const = lambda shape: pl.BlockSpec(shape, lambda i, o: (0,) * len(shape))
    in_specs = [pl.BlockSpec((NT, S, D), lambda i, o: (i, 0, 0))]
    for t in range(NT):
        in_specs.append(pl.BlockSpec((1, S, D), lambda i, o, t=t: (o[NT * i + t], 0, 0)))
    in_specs += [pl.BlockSpec((1, NT, S), lambda i, o: (i, 0, 0))] * 2
    consts = (cols, hid, maskcol) + weights
    in_specs += [const(c.shape) for c in consts]
    out_shape = [
        jax.ShapeDtypeStruct((tiles, S, D), BF),
        jax.ShapeDtypeStruct((tiles, S, D), F32),
        jax.ShapeDtypeStruct((2, FF, D), F32),
        jax.ShapeDtypeStruct((2, D, FF), F32),
        jax.ShapeDtypeStruct((2, D, 3 * D), F32),
        jax.ShapeDtypeStruct((2, D, D), F32),
        jax.ShapeDtypeStruct((24, D), F32),
    ]
    out_specs = [pl.BlockSpec((NT, S, D), lambda i, o: (i, 0, 0))] * 2
    out_specs += [const(o.shape) for o in out_shape[2:]]
    scratch = [
        pltpu.VMEM((2, 6, D, S), F32),
        pltpu.VMEM((D, S), F32),
        pltpu.VMEM((2, FF, S), F32),
        pltpu.VMEM((2, FF, D), F32),
        pltpu.VMEM((2, FF, D), F32),
        pltpu.VMEM((2, 3 * D, D), F32),
        pltpu.VMEM((2, D, D), F32),
        pltpu.VMEM((2, NT, HEADS, S, S), BF),
        pltpu.VMEM((2, 3 * D, L), BF),
        pltpu.VMEM((2, 8 * HEADS, L), F32),
        pltpu.VMEM((2, D, L), F32),
        pltpu.VMEM((2, FF, L), BF),
        pltpu.VMEM((2, FF, L), BF),
    ]
    return pl.pallas_call(
        kernel,
        grid_spec=pltpu.PrefetchScalarGridSpec(
            num_scalar_prefetch=1,
            grid=(steps,),
            in_specs=in_specs,
            out_specs=out_specs,
            scratch_shapes=scratch,
        ),
        out_shape=out_shape,
        compiler_params=pltpu.CompilerParams(
            dimension_semantics=("arbitrary",), vmem_limit_bytes=56 * 1024 * 1024
        ),
    )(inv_order, x, *([cot] * NT), seg.reshape(steps, NT, S), vis.reshape(steps, NT, S), *consts)


def prepare(mask_token, norm_gains, shift_terms, attn_in, attn_out, mlp_in, hidden_shift, mlp_out):
    rows = jnp.concatenate([norm_gains, shift_terms], axis=1)
    cols = jnp.broadcast_to(rows[..., None], (2, 6, D, S))
    hid = jnp.broadcast_to(hidden_shift[..., None], (2, FF, S))
    maskcol = jnp.broadcast_to(mask_token[:, None], (D, S))
    tr = lambda v: jnp.swapaxes(v, 1, 2)
    weights = (tr(attn_in), attn_in, tr(attn_out), attn_out, tr(mlp_in), mlp_in, tr(mlp_out), mlp_out)
    return cols, hid, maskcol, weights


def on_device(token_tiles, segment_ids, visible_flags, tile_order, mask_token, norm_gains, shift_terms,
              attn_in, attn_out, mlp_in, hidden_shift, mlp_out, cotangent):
    tiles = token_tiles.shape[2]
    full_shape = (1, 1, tiles, S, D)
    order = tile_order.reshape(tiles)
    spots = jnp.arange(tiles, dtype=jnp.int32)
    inv_order = jnp.sum(jnp.where(order[None, :] == spots[:, None], spots[None, :], 0), axis=1).astype(jnp.int32)
    cot = lax.all_to_all(cotangent.reshape(tiles, S, D), "dp", split_axis=0, concat_axis=0, tiled=True)
    cols, hid, maskcol, weights = prepare(
        mask_token, norm_gains, shift_terms, attn_in, attn_out, mlp_in, hidden_shift, mlp_out)
    dec, tg, g_m2, g_m1, g_wi, g_wo, rows = local_compute(
        token_tiles.reshape(tiles, S, D), segment_ids.reshape(tiles, S), visible_flags.reshape(tiles, S),
        inv_order, cot, cols, hid, maskcol, weights)
    decoded = lax.all_to_all(jnp.take(dec, order, axis=0), "dp", split_axis=0, concat_axis=0, tiled=True)
    g_m2, g_m1, g_wi, g_wo, rows = lax.psum((g_m2, g_m1, g_wi, g_wo, rows), ("dp", "group"))
    vec = rows[0:12].reshape(2, 6, D)
    return (
        decoded.reshape(full_shape),
        tg.reshape(full_shape),
        rows[20],
        vec[:, 0:2],
        vec[:, 2:6],
        g_wi,
        g_wo,
        g_m1,
        rows[12:20].reshape(2, FF),
        g_m2,
    )


def solution(mesh):
    tile5 = P("dp", "group", None, None, None)
    in_specs = (tile5, P("dp", "group", None, None), P("dp", "group", None, None), P("dp", "group", None),
                P(), P(), P(), P(), P(), P(), P(), P(), tile5)
    out_specs = (tile5, tile5) + (P(),) * 8
    return jax.shard_map(on_device, mesh=mesh, in_specs=in_specs, out_specs=out_specs, check_vma=False)
```

```python
import jax
import jax.numpy as jnp
from jax import lax
from jax.experimental import pallas as pl
from jax.experimental.pallas import tpu as pltpu
from jax.sharding import PartitionSpec as P

HEADS = 8
HEAD = 16
D = 128
FF = 512
S = 128
NT = 2
NG = 2
LAG_E = 3
LAG_D = 3
LAG_B = 3
L = NT * S
STEP = NT * NG
SMALL = 2 * FF + 4 * D
PACKED = SMALL + 64
EPS = 1e-5
LOG2E = 1.4426950408889634
LN2 = 0.6931471805599453
F32 = jnp.float32
BF = jnp.bfloat16


def nn(a, b):
    return lax.dot_general(a, b, (((1,), (0,)), ((), ())), preferred_element_type=F32)


def nt(a, b):
    return lax.dot_general(a, b, (((1,), (1,)), ((), ())), preferred_element_type=F32)


def wide(col):
    return jnp.concatenate([col] * NT, axis=1)


def fold(val):
    out = val[:, :S]
    for t in range(1, NT):
        out = out + val[:, t * S:(t + 1) * S]
    return out


def normalize(x):
    center = x - jnp.sum(x, axis=0, keepdims=True) * (1.0 / D)
    var = jnp.sum(center * center, axis=0, keepdims=True) * (1.0 / D)
    rstd = lax.rsqrt(var + EPS)
    return center * rstd, rstd


def norm_back(grad, xhat, rstd, gain):
    gx = grad * gain
    m1 = jnp.sum(gx, axis=0, keepdims=True) * (1.0 / D)
    m2 = jnp.sum(gx * xhat, axis=0, keepdims=True) * (1.0 / D)
    return (gx - m1 - xhat * m2) * rstd


def padded(rows, h):
    parts = []
    if h > 0:
        parts.append(jnp.zeros((HEAD * h, S), BF))
    parts.append(rows)
    if h < HEADS - 1:
        parts.append(jnp.zeros((D - HEAD * (h + 1), S), BF))
    return jnp.concatenate(parts, axis=0)


def pair_rhs(two, h):
    return jnp.concatenate([padded(two[0:HEAD], h), padded(two[HEAD:2 * HEAD], h + 1)], axis=1)


UNITS = [(t, h) for t in range(NT) for h in range(0, HEADS, 2)]


def layer_fwd(x, biases, w, sv):
    wi_t, wo_t, m1_t, m2_t, cols, hid = w["wi_t"], w["wo_t"], w["m1_t"], w["m2_t"], w["cols"], w["hid"]
    xhat0, rstd0 = normalize(x)
    sv["xhat0"][...] = xhat0.astype(BF)
    sv["rstd"][0:8, :] = jnp.broadcast_to(rstd0, (8, L))
    a = (xhat0 * wide(cols[0]) + wide(cols[2])).astype(BF)
    sv["a"][...] = a
    p = nn(wi_t[...], a)
    yield
    sv["p"][0:D, :] = (p[0:D] * (0.25 * LOG2E)).astype(BF)
    sv["p"][D:3 * D, :] = p[D:3 * D].astype(BF)
    yield
    ones = jnp.ones((HEAD, S), BF)
    keys = [jnp.transpose(sv["p"][D:2 * D, t * S:(t + 1) * S]) for t in range(NT)]
    n = len(UNITS)
    for i in range(n + 2):
        if i < n:
            t, h = UNITS[i]
            sl = slice(t * S, (t + 1) * S)
            sv["s"][i] = nn(keys[t], pair_rhs(sv["p"][HEAD * h:HEAD * (h + 2), sl], h))
        if 1 <= i <= n:
            t, h = UNITS[i - 1]
            for k in range(2):
                s = sv["s"][i - 1, :, k * S:(k + 1) * S] + biases[t]
                e = jnp.exp2(s - jnp.max(s, axis=0, keepdims=True)).astype(BF)
                sv["e"][t, :, (h + k) * S:(h + k + 1) * S] = e
        if i >= 2:
            t, h = UNITS[i - 2]
            sl = slice(t * S, (t + 1) * S)
            v = sv["p"][2 * D + HEAD * h:2 * D + HEAD * (h + 2), sl]
            o = nn(jnp.concatenate([v, ones], axis=0), sv["e"][t, :, h * S:(h + 2) * S])
            for k in range(2):
                kl = slice(k * S, (k + 1) * S)
                inv = 1.0 / o[2 * HEAD:2 * HEAD + 8, kl]
                sv["inv"][8 * (h + k):8 * (h + k) + 8, sl] = inv
                sv["o"][HEAD * (h + k):HEAD * (h + k + 1), sl] = (
                    o[HEAD * k:HEAD * (k + 1), kl] * jnp.concatenate([inv, inv], axis=0)).astype(BF)
        yield
    x1 = x + nn(wo_t[...], sv["o"][...]) + wide(cols[4])
    yield
    xhat1, rstd1 = normalize(x1)
    sv["xhat1"][...] = xhat1.astype(BF)
    sv["rstd"][8:16, :] = jnp.broadcast_to(rstd1, (8, L))
    b = (xhat1 * wide(cols[1]) + wide(cols[3])).astype(BF)
    sv["b"][...] = b
    yield
    hidden = None
    for i in range(5):
        last = hidden
        if i < 4:
            hidden = nn(m1_t[i * D:(i + 1) * D, :], b)
        if i >= 1:
            rows = slice((i - 1) * D, i * D)
            hv = last + wide(hid[rows, :])
            cdf = 0.5 * lax.erf(hv * 0.7071067811865476) + 0.5
            sv["u"][rows, :] = (hv * cdf).astype(BF)
            phi = jnp.exp2(hv * hv * (-0.5 * LOG2E)) * 0.3989422804014327
            sv["gp"][rows, :] = (cdf + hv * phi).astype(BF)
        yield
    return x1 + nn(m2_t[...], sv["u"][...]) + wide(cols[5])


def layer_bwd(g2, w, sv, acc):
    wi, wo, m1, m2, cols = w["wi"], w["wo"], w["m1"], w["m2"], w["cols"]
    a_vec, a_hid, a_wi, a_wo, a_m1, a_m2 = acc
    gz = g2.astype(BF)
    a_vec[5] += fold(g2)
    gu = None
    for i in range(5):
        last = gu
        if i < 4:
            rows = slice(i * D, (i + 1) * D)
            gu = nn(m2[rows, :], gz)
            a_m2[rows, :] += nt(sv["u"][rows, :], gz)
        if i >= 1:
            rows = slice((i - 1) * D, i * D)
            gh = last * sv["gp"][rows, :].astype(F32)
            a_hid[rows, :] += fold(gh)
            ghb = gh.astype(BF)
            sv["gh"][rows, :] = ghb
            a_m1[rows, :] += nt(ghb, sv["b"][...])
        yield
    gb = nn(m1[...], sv["gh"][...])
    yield
    xhat1 = sv["xhat1"][...].astype(F32)
    a_vec[1] += fold(gb * xhat1)
    a_vec[3] += fold(gb)
    g1 = g2 + norm_back(gb, xhat1, sv["rstd"][8:9, :], wide(cols[1]))
    gy = g1.astype(BF)
    a_vec[4] += fold(g1)
    yield
    a_wo[...] += nt(sv["o"][...], gy)
    go = nn(wo[...], gy)
    yield
    values = [jnp.transpose(sv["p"][2 * D:3 * D, t * S:(t + 1) * S]) for t in range(NT)]
    n = len(UNITS)
    gobs, rs = {}, {}
    for i in range(n + 2):
        if i < n:
            t, h = UNITS[i]
            sl = slice(t * S, (t + 1) * S)
            parts = []
            for k in (h, h + 1):
                hs = slice(HEAD * k, HEAD * (k + 1))
                inv = sv["inv"][8 * k:8 * k + 8, sl]
                gob = (go[hs, sl] * jnp.concatenate([inv, inv], axis=0)).astype(BF)
                parts.append(gob)
                rs[t, k] = jnp.sum(gob.astype(F32) * sv["o"][hs, sl].astype(F32), axis=0, keepdims=True)
            gobs[i] = jnp.concatenate(parts, axis=0)
            sv["s"][i] = nn(values[t], pair_rhs(gobs[i], h))
        if 1 <= i <= n:
            t, h = UNITS[i - 1]
            for k in range(2):
                kl = slice(k * S, (k + 1) * S)
                e = sv["e"][t, :, (h + k) * S:(h + k + 1) * S].astype(F32)
                sv["gs"][i - 1, :, kl] = (e * (sv["s"][i - 1, :, kl] - rs[t, h + k])).astype(BF)
        if i >= 2:
            t, h = UNITS[i - 2]
            sl = slice(t * S, (t + 1) * S)
            e2 = jnp.concatenate([sv["e"][t, :, (h + k) * S:(h + k + 1) * S] for k in range(2)], axis=0)
            s2 = jnp.concatenate([sv["gs"][i - 2, :, k * S:(k + 1) * S] for k in range(2)], axis=0)
            pv = nt(gobs[i - 2], e2)
            pq = nn(sv["p"][D + HEAD * h:D + HEAD * (h + 2), sl], sv["gs"][i - 2])
            pk = nt(sv["p"][HEAD * h:HEAD * (h + 2), sl], s2)
            for k in range(2):
                kr = slice(HEAD * k, HEAD * (k + 1))
                kl = slice(k * S, (k + 1) * S)
                at = HEAD * (h + k)
                sv["gpk"][at:at + HEAD, sl] = (pq[kr, kl] * 0.25).astype(BF)
                sv["gpk"][D + at:D + at + HEAD, sl] = (pk[kr, kl] * LN2).astype(BF)
                sv["gpk"][2 * D + at:2 * D + at + HEAD, sl] = pv[kr, kl].astype(BF)
        yield
    gp = sv["gpk"][...]
    ga = nn(wi[...], gp)
    a_wi[...] += nt(gp, sv["a"][...])
    yield
    xhat0 = sv["xhat0"][...].astype(F32)
    a_vec[0] += fold(ga * xhat0)
    a_vec[2] += fold(ga)
    return g1 + norm_back(ga, xhat0, sv["rstd"][0:1, :], wide(cols[0]))


def masks(seg_ref, vis_ref, first, decoder):
    rows_i = lax.broadcasted_iota(jnp.int32, (S, S), 0)
    cols_i = lax.broadcasted_iota(jnp.int32, (S, S), 1)
    diag = rows_i == cols_i
    out = []
    for t in range(NT):
        seg = seg_ref[0, first + t:first + t + 1, :]
        key = jnp.where(seg >= 0, seg, -2)
        if not decoder:
            key = jnp.where(vis_ref[0, first + t:first + t + 1, :] == 1, key, -2)
        key_k = jnp.transpose(jnp.broadcast_to(key, (S, S)).astype(F32))
        out.append(jnp.where((key_k == seg.astype(F32)) | diag, 0.0, -1e30))
    return out


def identity():
    rows_i = lax.broadcasted_iota(jnp.int32, (S, S), 0)
    cols_i = lax.broadcasted_iota(jnp.int32, (S, S), 1)
    return (rows_i == cols_i).astype(F32).astype(BF)


def drive(gens, lag):
    live = [True] * len(gens)
    tick = 0
    while any(live):
        for j, gen in enumerate(gens):
            if live[j] and tick >= lag * j:
                try:
                    next(gen)
                except StopIteration:
                    live[j] = False
        tick += 1


SAVED = {
    "p": ((3 * D, L), BF),
    "e": ((NT, S, HEADS * S), BF),
    "inv": ((8 * HEADS, L), F32),
    "o": ((D, L), BF),
    "u": ((FF, L), BF),
    "gp": ((FF, L), BF),
    "xhat0": ((D, L), BF),
    "xhat1": ((D, L), BF),
    "a": ((D, L), BF),
    "b": ((D, L), BF),
    "rstd": ((16, L), F32),
}
SCORES = {"s": ((len(UNITS), S, 2 * S), F32)}
BACK = {
    "gs": ((len(UNITS), S, 2 * S), BF),
    "gh": ((FF, L), BF),
    "gpk": ((3 * D, L), BF),
}
RAW = ("gains", "shifts", "hidden", "wi", "wo", "m1", "m2")
PREP = {
    "cols": ((6, D, S), F32),
    "hid": ((FF, S), F32),
    "wi_t": ((3 * D, D), BF),
    "wo_t": ((D, D), BF),
    "m1_t": ((FF, D), BF),
    "m2_t": ((D, FF), BF),
}


def spread_row(row):
    return jnp.transpose(jnp.broadcast_to(row, (S, D)))


def prep_weights(l, raw, prep, forward):
    raw = dict(zip(RAW, raw))
    prep = dict(zip(PREP, prep))

    @pl.when(pl.program_id(0) == 0)
    def _():
        for j in range(2):
            prep["cols"][j] = spread_row(raw["gains"][l, j:j + 1, :])
        for j in range(4):
            prep["cols"][2 + j] = spread_row(raw["shifts"][l, j:j + 1, :])
        if forward:
            for j in range(4):
                rows = slice(j * D, (j + 1) * D)
                prep["hid"][rows, :] = spread_row(raw["hidden"][l:l + 1, rows])
                prep["m1_t"][rows, :] = jnp.transpose(raw["m1"][l, :, rows])
                prep["m2_t"][:, rows] = jnp.transpose(raw["m2"][l, rows, :])
            for j in range(3):
                rows = slice(j * D, (j + 1) * D)
                prep["wi_t"][rows, :] = jnp.transpose(raw["wi"][l, :, rows])
            prep["wo_t"][...] = jnp.transpose(raw["wo"][l])

    return prep | {name: raw[name].at[l] for name in ("wi", "wo", "m1", "m2")}


def scratch_of(table):
    return [pltpu.VMEM((NG,) + shape, dt) for shape, dt in table.values()]


def prep_scratch():
    return [pltpu.VMEM(shape, dt) for shape, dt in PREP.values()]


def views(names, refs, g):
    return {name: ref.at[g] for name, ref in zip(names, refs)}


def encode_kernel(x_ref, seg_ref, vis_ref, *rest):
    raw, rest = rest[:len(RAW)], rest[len(RAW):]
    enc_ref = rest[0]
    saved = rest[1:1 + len(SAVED)]
    score = rest[1 + len(SAVED):1 + len(SAVED) + len(SCORES)]
    w = prep_weights(0, raw, rest[1 + len(SAVED) + len(SCORES):], True)
    eye = identity()

    def group(g):
        sv = views(SAVED, saved, g) | views(SCORES, score, g)
        bias = masks(seg_ref, vis_ref, NT * g, False)
        x = jnp.concatenate([nt(eye, x_ref[NT * g + t]) for t in range(NT)], axis=1)
        yield
        out = yield from layer_fwd(x, bias, w, sv)
        enc_ref[g] = out.astype(BF)

    drive([group(g) for g in range(NG)], LAG_E)


def zero_first(refs):
    @pl.when(pl.program_id(0) == 0)
    def _():
        for ref in refs:
            ref[...] = jnp.zeros_like(ref)


ACC = [
    ((6, D, S), F32),
    ((FF, S), F32),
    ((3 * D, D), F32),
    ((D, D), F32),
    ((FF, D), F32),
    ((FF, D), F32),
]


def finish(acc, out, a_mask=None):
    a_vec, a_hid, a_wi, a_wo, a_m1, a_m2 = acc

    @pl.when(pl.program_id(0) == pl.num_programs(0) - 1)
    def _():
        out[0:FF, :] = a_m2[...]
        for j in range(4):
            rows = slice(j * D, (j + 1) * D)
            out[FF + j * D:FF + (j + 1) * D, :] = jnp.transpose(a_m1[rows, :])
        for j in range(3):
            rows = slice(j * D, (j + 1) * D)
            out[2 * FF + j * D:2 * FF + (j + 1) * D, :] = jnp.transpose(a_wi[rows, :])
        out[2 * FF + 3 * D:SMALL, :] = a_wo[...]
        out[SMALL:PACKED, :] = jnp.zeros((PACKED - SMALL, D), F32)
        for j in range(6):
            out[SMALL + j:SMALL + j + 1, :] = jnp.sum(jnp.transpose(a_vec[j]), axis=0, keepdims=True)
        for j in range(4):
            out[SMALL + 6 + j:SMALL + 7 + j, :] = jnp.sum(
                jnp.transpose(a_hid[j * D:(j + 1) * D]), axis=0, keepdims=True)
        if a_mask is not None:
            out[SMALL + 10:SMALL + 11, :] = jnp.sum(jnp.transpose(a_mask[...]), axis=0, keepdims=True)


def decode_kernel(inv_order, enc_ref, *rest):
    cots = rest[:STEP]
    seg_ref, vis_ref, mask_row = rest[STEP:STEP + 3]
    rest = rest[STEP + 3:]
    raw, rest = rest[:len(RAW)], rest[len(RAW):]
    dec_out, ge_ref, out_ref = rest[:3]
    rest = rest[3:]
    acc, rest = rest[:len(ACC)], rest[len(ACC):]
    a_mask, maskcol, dec_ref, sems = rest[:4]
    rest = rest[4:]
    w = prep_weights(1, raw, rest[:len(PREP)], True)
    scr = rest[len(PREP):]
    step = pl.program_id(0)
    slot = lax.rem(step, 2)

    @pl.when(step == 0)
    def _():
        maskcol[...] = spread_row(mask_row[0:1, :])

    def copies(at, where):
        return [
            pltpu.make_async_copy(dec_ref.at[where, t], dec_out.at[inv_order[STEP * at + t]], sems.at[where, t])
            for t in range(STEP)
        ]

    @pl.when(step >= 2)
    def _():
        for copy in copies(step - 2, slot):
            copy.wait()

    zero_first(acc + (a_mask,))
    eye = identity()
    table = list(SAVED) + list(SCORES) + list(BACK)

    def group(g):
        sv = views(table, scr, g)
        bias = masks(seg_ref, vis_ref, NT * g, True)
        shown = jnp.concatenate([vis_ref[0, NT * g + t:NT * g + t + 1, :] for t in range(NT)], axis=1) == 1
        x = jnp.where(shown, enc_ref[g].astype(F32), wide(maskcol[...]))
        yield
        out = yield from layer_fwd(x, bias, w, sv)
        outb = out.astype(BF)
        for t in range(NT):
            dec_ref[slot, NT * g + t] = nt(eye, outb[:, t * S:(t + 1) * S]).astype(BF)
        yield
        grad = jnp.concatenate([nt(eye, cots[NT * g + t][0]) for t in range(NT)], axis=1)
        yield
        grad = yield from layer_bwd(grad, w, sv, acc)
        a_mask[...] += fold(jnp.where(shown, 0.0, grad))
        ge_ref[g] = jnp.where(shown, grad, 0.0).astype(BF)

    drive([group(g) for g in range(NG)], LAG_D)
    for copy in copies(step, slot):
        copy.start()

    @pl.when(step == pl.num_programs(0) - 1)
    def _():
        for copy in copies(step - 1, 1 - slot) + copies(step, slot):
            copy.wait()

    finish(acc, out_ref, a_mask)


def back_kernel(ge_ref, *rest):
    saved = rest[:len(SAVED)]
    rest = rest[len(SAVED):]
    raw, rest = rest[:len(RAW)], rest[len(RAW):]
    tg_ref, out_ref = rest[:2]
    acc = rest[2:2 + len(ACC)]
    w = prep_weights(0, raw, rest[2 + len(ACC):2 + len(ACC) + len(PREP)], False)
    scr = rest[2 + len(ACC) + len(PREP):]
    zero_first(acc)
    table = list(SCORES) + list(BACK)

    def group(g):
        sv = views(SAVED, saved, g) | views(table, scr, g)
        grad = ge_ref[g].astype(F32)
        yield
        grad = yield from layer_bwd(grad, w, sv, acc)
        for t in range(NT):
            tg_ref[NT * g + t] = jnp.transpose(grad[:, t * S:(t + 1) * S])

    drive([group(g) for g in range(NG)], LAG_B)
    finish(acc, out_ref)


def const_spec(arr):
    return pl.BlockSpec(arr.shape, lambda *_: (0,) * arr.ndim)


def step_spec(shape):
    return pl.BlockSpec(shape, lambda i, *_: (i,) + (0,) * (len(shape) - 1))


PARAMS = pltpu.CompilerParams(dimension_semantics=("arbitrary",), vmem_limit_bytes=60 * 1024 * 1024)
GRADS = [jax.ShapeDtypeStruct((PACKED, D), F32)]


def cost(flops, nbytes):
    return pl.CostEstimate(flops=flops, bytes_accessed=nbytes, transcendentals=0)


def run_encode(x, seg, vis, w):
    tiles = x.shape[0]
    groups, steps = tiles // NT, tiles // STEP
    ops = list(w)
    out_shape = [jax.ShapeDtypeStruct((groups, D, L), BF)]
    out_shape += [jax.ShapeDtypeStruct((groups,) + shape, dt) for shape, dt in SAVED.values()]
    return pl.pallas_call(
        encode_kernel,
        grid=(steps,),
        in_specs=[step_spec((STEP, S, D)), step_spec((1, STEP, S)), step_spec((1, STEP, S))] + [const_spec(o) for o in ops],
        out_specs=[step_spec((NG,) + o.shape[1:]) for o in out_shape],
        out_shape=out_shape,
        scratch_shapes=scratch_of(SCORES) + prep_scratch(),
        cost_estimate=cost(20 * 10**9, 60 * 10**6),
        compiler_params=PARAMS,
    )(x, seg.reshape(steps, STEP, S), vis.reshape(steps, STEP, S), *ops)


def run_decode(inv_order, enc, cot, seg, vis, mask_row, w):
    tiles = cot.shape[0]
    groups, steps = tiles // NT, tiles // STEP
    ops = [mask_row] + list(w)
    cot_specs = [pl.BlockSpec((1, S, D), lambda i, o, t=t: (o[STEP * i + t], 0, 0)) for t in range(STEP)]
    out_shape = [jax.ShapeDtypeStruct((tiles, S, D), BF), jax.ShapeDtypeStruct((groups, D, L), BF)] + GRADS
    return pl.pallas_call(
        decode_kernel,
        grid_spec=pltpu.PrefetchScalarGridSpec(
            num_scalar_prefetch=1,
            grid=(steps,),
            in_specs=[step_spec((NG, D, L))] + cot_specs + [step_spec((1, STEP, S))] * 2 + [const_spec(o) for o in ops],
            out_specs=[pl.BlockSpec(memory_space=pl.ANY), step_spec((NG, D, L))] + [const_spec(o) for o in GRADS],
            scratch_shapes=[pltpu.VMEM(shape, dt) for shape, dt in ACC] + [pltpu.VMEM((D, S), F32)] * 2
            + [pltpu.VMEM((2, STEP, S, D), BF), pltpu.SemaphoreType.DMA((2, STEP))]
            + prep_scratch() + scratch_of(SAVED) + scratch_of(SCORES) + scratch_of(BACK),
        ),
        out_shape=out_shape,
        cost_estimate=cost(40 * 10**9, 10 * 10**6),
        compiler_params=PARAMS,
    )(inv_order, enc, *([cot] * STEP), seg.reshape(steps, STEP, S), vis.reshape(steps, STEP, S), *ops)


def run_back(ge, saved, w):
    groups = ge.shape[0]
    steps = groups // NG
    ops = list(w)
    out_shape = [jax.ShapeDtypeStruct((groups * NT, S, D), F32)] + GRADS
    return pl.pallas_call(
        back_kernel,
        grid=(steps,),
        in_specs=[step_spec((NG, D, L))] + [step_spec((NG,) + s.shape[1:]) for s in saved] + [const_spec(o) for o in ops],
        out_specs=[step_spec((STEP, S, D))] + [const_spec(o) for o in GRADS],
        out_shape=out_shape,
        scratch_shapes=[pltpu.VMEM(shape, dt) for shape, dt in ACC] + prep_scratch() + scratch_of(SCORES) + scratch_of(BACK),
        cost_estimate=cost(20 * 10**9, 60 * 10**6),
        compiler_params=PARAMS,
    )(ge, *saved, *ops)


def unpack_kernel(core_ref, mine, other, g_m2, g_m1, g_wi, g_wo, g_gain, g_shift, g_hid, g_mask):
    core = core_ref[0]

    def write(src, l):
        g_m2[l] = src[0:FF, :].astype(F32)
        for j in range(4):
            g_m1[l, :, j * D:(j + 1) * D] = src[FF + j * D:FF + (j + 1) * D, :].astype(F32)
        for j in range(3):
            g_wi[l, :, j * D:(j + 1) * D] = src[2 * FF + j * D:2 * FF + (j + 1) * D, :].astype(F32)
        g_wo[l] = src[2 * FF + 3 * D:SMALL, :].astype(F32)
        rows = src[SMALL:SMALL + 16, :].astype(F32)
        g_gain[l] = rows[0:2]
        g_shift[l] = rows[2:6]
        for j in range(4):
            g_hid[l:l + 1, j * D:(j + 1) * D] = rows[6 + j:7 + j]
        if l == 1:
            g_mask[...] = rows[10:11]

    @pl.when(core == 0)
    def _():
        write(mine, 0)
        write(other, 1)

    @pl.when(core == 1)
    def _():
        write(other, 0)
        write(mine, 1)


def unpack(core, mine, other):
    shapes = [(2, FF, D), (2, D, FF), (2, D, 3 * D), (2, D, D), (2, 2, D), (2, 4, D), (2, FF), (1, D)]
    return pl.pallas_call(
        unpack_kernel,
        grid_spec=pltpu.PrefetchScalarGridSpec(
            num_scalar_prefetch=1,
            grid=(1,),
            in_specs=[const_spec(mine), const_spec(other)],
            out_specs=[pl.BlockSpec(sh, lambda *_, n=len(sh): (0,) * n) for sh in shapes],
        ),
        out_shape=[jax.ShapeDtypeStruct(sh, F32) for sh in shapes],
        compiler_params=PARAMS,
    )(core.reshape(1).astype(jnp.int32), mine, other)


def swap(value, axis, bits, size):
    return lax.ppermute(value, axis, [(i, i ^ bits) for i in range(size)])


def split(value, bit):
    half = value.shape[0] // 2
    keep = lax.dynamic_slice_in_dim(value, bit * half, half, axis=0)
    send = lax.dynamic_slice_in_dim(value, (1 - bit) * half, half, axis=0)
    return keep, send.astype(BF)


def join(mine, other, bit):
    return jnp.where(bit == 0, jnp.concatenate([mine, other], axis=0), jnp.concatenate([other, mine], axis=0))


def reduce_all(first, second, n_dp, n_group):
    core = lax.axis_index("dp") % 2
    x = lax.axis_index("group")
    keep = jnp.where(core == 0, first, second)
    send = jnp.where(core == 0, second, first).astype(BF)
    value = keep + swap(send, "dp", 1, n_dp).astype(F32)
    for bits, bit in ((3, x // 2), (1, x % 2)):
        keep, send = split(value, bit)
        value = keep + swap(send, "group", bits, n_group).astype(F32)
    for bits in (2, 6, 8, 24):
        value = value + swap(value.astype(BF), "dp", bits, n_dp).astype(F32)
    value = value.astype(BF)
    for bits, bit in ((1, x % 2), (3, x // 2)):
        value = join(value, swap(value, "group", bits, n_group), bit)
    other = swap(value, "dp", 1, n_dp)
    return core, value, other


def on_device(token_tiles, segment_ids, visible_flags, tile_order, mask_token, norm_gains, shift_terms,
              attn_in, attn_out, mlp_in, hidden_shift, mlp_out, cotangent):
    tiles = token_tiles.shape[2]
    full_shape = (1, 1, tiles, S, D)
    order = tile_order.reshape(tiles)
    spots = jnp.arange(tiles, dtype=jnp.int32)
    inv_order = jnp.sum(jnp.where(order[None, :] == spots[:, None], spots[None, :], 0), axis=1).astype(jnp.int32)
    cot = lax.all_to_all(cotangent.reshape(tiles, S, D), "dp", split_axis=0, concat_axis=0, tiled=True)
    w = (norm_gains, shift_terms, hidden_shift, attn_in, attn_out, mlp_in, mlp_out)
    seg, vis = segment_ids.reshape(tiles, S), visible_flags.reshape(tiles, S)
    enc, *saved = run_encode(token_tiles.reshape(tiles, S, D), seg, vis, w)
    dec, ge, packed1 = run_decode(inv_order, enc, cot, seg, vis, mask_token.reshape(1, D), w)
    decoded = lax.all_to_all(dec, "dp", split_axis=0, concat_axis=0, tiled=True)
    tg, packed0 = run_back(ge, saved, w)
    n_dp = lax.axis_size("dp")
    if n_dp == 32:
        decoded, packed0 = lax.optimization_barrier((decoded, packed0))
        core, mine, other = reduce_all(packed0, packed1, n_dp, lax.axis_size("group"))
    else:
        core, mine, other = jnp.int32(0), packed0.astype(BF), packed1.astype(BF)
    g_m2, g_m1, g_wi, g_wo, g_gain, g_shift, g_hid, g_mask = unpack(core, mine, other)
    return (
        decoded.reshape(full_shape),
        tg.reshape(full_shape),
        g_mask.reshape(D),
        g_gain,
        g_shift,
        g_wi,
        g_wo,
        g_m1,
        g_hid,
        g_m2,
    )


def solution(mesh):
    tile5 = P("dp", "group", None, None, None)
    in_specs = (tile5, P("dp", "group", None, None), P("dp", "group", None, None), P("dp", "group", None),
                P(), P(), P(), P(), P(), P(), P(), P(), tile5)
    out_specs = (tile5, tile5) + (P(),) * 8
    return jax.shard_map(on_device, mesh=mesh, in_specs=in_specs, out_specs=out_specs, check_vma=False)
```

```python
import jax
import jax.numpy as jnp
from jax import lax
from jax.experimental import pallas as pl
from jax.experimental.pallas import tpu as pltpu
from jax.sharding import PartitionSpec as P

HEADS = 8
HEAD = 16
D = 128
FF = 512
S = 128
NT = 2
NG_E = 8
TURN_E = 2
TURN_D = 2
TURN_B = 2
NG_D = 8
NG_B = 4
L = NT * S
SMALL = 2 * FF + 4 * D
PACKED = SMALL + 64
EPS = 1e-5
LOG2E = 1.4426950408889634
LN2 = 0.6931471805599453
F32 = jnp.float32
BF = jnp.bfloat16


def nn(a, b):
    return lax.dot_general(a, b, (((1,), (0,)), ((), ())), preferred_element_type=F32)


def nt(a, b):
    return lax.dot_general(a, b, (((1,), (1,)), ((), ())), preferred_element_type=F32)


def wide(col):
    return jnp.concatenate([col] * NT, axis=1)


def fold(val):
    out = val[:, :S]
    for t in range(1, NT):
        out = out + val[:, t * S:(t + 1) * S]
    return out


def normalize(x):
    center = x - jnp.sum(x, axis=0, keepdims=True) * (1.0 / D)
    var = jnp.sum(center * center, axis=0, keepdims=True) * (1.0 / D)
    rstd = lax.rsqrt(var + EPS)
    return center * rstd, rstd


def norm_back(grad, xhat, rstd, gain):
    gx = grad * gain
    m1 = jnp.sum(gx, axis=0, keepdims=True) * (1.0 / D)
    m2 = jnp.sum(gx * xhat, axis=0, keepdims=True) * (1.0 / D)
    return (gx - m1 - xhat * m2) * rstd


def padded(rows, h):
    parts = []
    if h > 0:
        parts.append(jnp.zeros((HEAD * h, S), BF))
    parts.append(rows)
    if h < HEADS - 1:
        parts.append(jnp.zeros((D - HEAD * (h + 1), S), BF))
    return jnp.concatenate(parts, axis=0)


def pair_rhs(two, h):
    return jnp.concatenate([padded(two[0:HEAD], h), padded(two[HEAD:2 * HEAD], h + 1)], axis=1)


def flip_pair(two):
    return jnp.concatenate([jnp.transpose(two[:, 0:S]), jnp.transpose(two[:, S:2 * S])], axis=1)


def pair_lhs(two):
    zero = jnp.zeros((HEAD, S), BF)
    return jnp.concatenate(
        [jnp.concatenate([two[0:HEAD], zero], axis=1), jnp.concatenate([zero, two[HEAD:2 * HEAD]], axis=1)], axis=0)


UNITS = [(t, h) for t in range(NT) for h in range(0, HEADS, 2)]


def mix_values(sv, t, h):
    sl = slice(t * S, (t + 1) * S)
    v = sv["p"][2 * D + HEAD * h:2 * D + HEAD * (h + 2), sl]
    o = nn(jnp.concatenate([v, jnp.ones((HEAD, S), BF)], axis=0), sv["e"][t, :, h * S:(h + 2) * S])
    totals = []
    for k in range(2):
        kl = slice(k * S, (k + 1) * S)
        totals.append(o[2 * HEAD:2 * HEAD + 8, kl])
        inv = 1.0 / totals[k]
        sv["inv"][8 * (h + k):8 * (h + k) + 8, sl] = inv
        sv["o"][HEAD * (h + k):HEAD * (h + k + 1), sl] = (
            o[HEAD * k:HEAD * (k + 1), kl] * jnp.concatenate([inv, inv], axis=0)).astype(BF)
    return totals


def redo_shifted(low, high, group_view, group_bias, ng):
    safe = (jnp.min(low) > 2.0 ** -60) & (jnp.max(high) < 2.0 ** 60)

    @pl.when(jnp.logical_not(safe))
    def _():
        def one(g, carry):
            sv = group_view(g)
            biases = group_bias(g)
            for t, h in UNITS:
                sl = slice(t * S, (t + 1) * S)
                keys = jnp.transpose(sv["p"][D:2 * D, sl])
                scores = nn(keys, pair_rhs(sv["p"][HEAD * h:HEAD * (h + 2), sl], h))
                for k in range(2):
                    part = scores[:, k * S:(k + 1) * S] + biases[t]
                    e = jnp.exp2(part - jnp.max(part, axis=0, keepdims=True))
                    sv["e"][t, :, (h + k) * S:(h + k + 1) * S] = e.astype(BF)
                mix_values(sv, t, h)
            return carry

        lax.fori_loop(0, ng, one, 0)


def layer_fwd(x, biases, w, sv, share):
    per_turn = share["per_turn"]
    wi_t, wo_t, m1_t, m2_t, cols, hid = w["wi_t"], w["wo_t"], w["m1_t"], w["m2_t"], w["cols"], w["hid"]
    xhat0, rstd0 = normalize(x)
    sv["xhat0"][...] = xhat0.astype(BF)
    sv["rstd"][0:8, :] = jnp.broadcast_to(rstd0, (8, L))
    a = (xhat0 * wide(cols[0]) + wide(cols[2])).astype(BF)
    sv["a"][...] = a
    p = nn(wi_t[...], a)
    yield
    sv["p"][0:D, :] = (p[0:D] * (0.25 * LOG2E)).astype(BF)
    sv["p"][D:3 * D, :] = p[D:3 * D].astype(BF)
    yield
    keys = [jnp.transpose(sv["p"][D:2 * D, t * S:(t + 1) * S]) for t in range(NT)]
    n = len(UNITS)
    for turn in range(0, n + per_turn, per_turn):
        for t, h in UNITS[turn:turn + per_turn]:
            scores = nn(keys[t], pair_rhs(sv["p"][HEAD * h:HEAD * (h + 2), t * S:(t + 1) * S], h))
            for k in range(2):
                e = jnp.exp2(scores[:, k * S:(k + 1) * S] + biases[t])
                sv["e"][t, :, (h + k) * S:(h + k + 1) * S] = e.astype(BF)
        for t, h in UNITS[max(turn - per_turn, 0):turn]:
            for total in mix_values(sv, t, h):
                share["low"] = total if share["low"] is None else jnp.minimum(share["low"], total)
                share["high"] = total if share["high"] is None else jnp.maximum(share["high"], total)
        yield
    if share["last"] is sv:
        share["redo"](share["low"], share["high"])
    yield
    x1 = x + nn(wo_t[...], sv["o"][...]) + wide(cols[4])
    yield
    xhat1, rstd1 = normalize(x1)
    sv["xhat1"][...] = xhat1.astype(BF)
    sv["rstd"][8:16, :] = jnp.broadcast_to(rstd1, (8, L))
    b = (xhat1 * wide(cols[1]) + wide(cols[3])).astype(BF)
    sv["b"][...] = b
    yield
    hidden = None
    for i in range(5):
        last = hidden
        if i < 4:
            hidden = nn(m1_t[i * D:(i + 1) * D, :], b)
        if i >= 1:
            rows = slice((i - 1) * D, i * D)
            hv = last + wide(hid[rows, :])
            arg = hv * 0.7071067811865476
            cdf2 = lax.erf(arg) + 1.0
            sv["u"][rows, :] = (hv * cdf2).astype(BF)
            bell = jnp.exp2(arg * arg * -LOG2E)
            sv["gp"][rows, :] = (cdf2 + arg * 1.1283791670955126 * bell).astype(BF)
        yield
    return x1 + nn(m2_t[...], sv["u"][...]) + wide(cols[5])


def lanes(views, name):
    return jnp.concatenate([sv[name][...] for sv in views], axis=1)


def layer_bwd(g2, w, sv, acc, share):
    wi, wo, m1, m2, cols = w["wi"], w["wo"], w["m1"], w["m2_h"], w["cols"]
    a_vec, a_wi, a_wo, a_m1, a_m2 = acc
    views = share["views"]
    per_turn = share["per_turn"]
    last = views[-1] is sv
    n = len(UNITS)
    gz = g2.astype(BF)
    sv["gz"][...] = gz
    gu = None
    for i in range(5):
        done = gu
        if i < 4:
            gu = nn(m2[i * D:(i + 1) * D, :], gz)
        if i >= 1:
            rows = slice((i - 1) * D, i * D)
            sv["gh"][rows, :] = (done * sv["gp"][rows, :].astype(F32)).astype(BF)
        yield
    gb = nn(m1[...], sv["gh"][...])
    yield
    if last:
        width = L * len(views)
        a_m2[...] += nt(jnp.concatenate([lanes(views, "u"), jnp.ones((HEAD, width), BF)], axis=0), lanes(views, "gz"))
    yield
    if last:
        a_m1[...] += nt(lanes(views, "gh"), jnp.concatenate([lanes(views, "b"), jnp.ones((D, width), BF)], axis=0))
    yield
    xhat1 = sv["xhat1"][...].astype(F32)
    a_vec[1] += fold(gb * xhat1)
    a_vec[3] += fold(gb)
    g1 = g2 + norm_back(gb, xhat1, sv["rstd"][8:9, :], wide(cols[1]))
    gy = g1.astype(BF)
    sv["gy"][...] = gy
    yield
    go = nn(wo[...], gy)
    yield
    if last:
        a_wo[...] += nt(jnp.concatenate([lanes(views, "o"), jnp.ones((HEAD, width), BF)], axis=0), lanes(views, "gy"))
    values = [jnp.transpose(sv["p"][2 * D:3 * D, t * S:(t + 1) * S]) for t in range(NT)]
    gobs = {}
    for turn in range(0, n + per_turn, per_turn):
        for i in range(turn, min(turn + per_turn, n)):
            t, h = UNITS[i]
            sl = slice(t * S, (t + 1) * S)
            parts, rs = [], []
            for k in (h, h + 1):
                hs = slice(HEAD * k, HEAD * (k + 1))
                inv = sv["inv"][8 * k:8 * k + 8, sl]
                gob = (go[hs, sl] * jnp.concatenate([inv, inv], axis=0)).astype(BF)
                parts.append(gob)
                rs.append(jnp.sum(gob.astype(F32) * sv["o"][hs, sl].astype(F32), axis=0, keepdims=True))
            gobs[i] = jnp.concatenate(parts, axis=0)
            gf = nn(values[t], pair_rhs(gobs[i], h))
            for k in range(2):
                kl = slice(k * S, (k + 1) * S)
                e = sv["e"][t, :, (h + k) * S:(h + k + 1) * S].astype(F32)
                sv["gs"][i, :, kl] = (e * (gf[:, kl] - rs[k])).astype(BF)
        for i in range(max(turn - per_turn, 0), turn):
            t, h = UNITS[i]
            sl = slice(t * S, (t + 1) * S)
            pv = nn(gobs[i], flip_pair(sv["e"][t, :, h * S:(h + 2) * S]))
            pq = nn(sv["p"][D + HEAD * h:D + HEAD * (h + 2), sl], sv["gs"][i])
            pk = nn(sv["p"][HEAD * h:HEAD * (h + 2), sl], flip_pair(sv["gs"][i]))
            for k in range(2):
                kr = slice(HEAD * k, HEAD * (k + 1))
                kl = slice(k * S, (k + 1) * S)
                at = HEAD * (h + k)
                sv["gpk"][at:at + HEAD, sl] = (pq[kr, kl] * 0.25).astype(BF)
                sv["gpk"][D + at:D + at + HEAD, sl] = (pk[kr, kl] * LN2).astype(BF)
                sv["gpk"][2 * D + at:2 * D + at + HEAD, sl] = pv[kr, kl].astype(BF)
        yield
    ga = nn(wi[...], sv["gpk"][...])
    yield
    if last:
        a_wi[...] += nt(lanes(views, "gpk"), lanes(views, "a"))
    xhat0 = sv["xhat0"][...].astype(F32)
    a_vec[0] += fold(ga * xhat0)
    a_vec[2] += fold(ga)
    return g1 + norm_back(ga, xhat0, sv["rstd"][0:1, :], wide(cols[0]))


def masks(seg_ref, vis_ref, first, decoder):
    rows_i = lax.broadcasted_iota(jnp.int32, (S, S), 0)
    cols_i = lax.broadcasted_iota(jnp.int32, (S, S), 1)
    diag = rows_i == cols_i
    out = []
    for t in range(NT):
        seg = seg_ref[0, pl.ds(first + t, 1), :]
        key = jnp.where(seg >= 0, seg, -2)
        if not decoder:
            key = jnp.where(vis_ref[0, pl.ds(first + t, 1), :] == 1, key, -2)
        key_k = jnp.transpose(jnp.broadcast_to(key, (S, S)).astype(F32))
        out.append(jnp.where((key_k == seg.astype(F32)) | diag, 0.0, -1e30))
    return out


def drive(gens):
    gens = list(gens)
    while gens:
        alive = []
        for gen in gens:
            try:
                next(gen)
                alive.append(gen)
            except StopIteration:
                pass
        gens = alive


SAVED = {
    "p": ((3 * D, L), BF),
    "e": ((NT, S, HEADS * S), BF),
    "inv": ((8 * HEADS, L), F32),
    "o": ((D, L), BF),
    "u": ((FF, L), BF),
    "gp": ((FF, L), BF),
    "xhat0": ((D, L), BF),
    "xhat1": ((D, L), BF),
    "a": ((D, L), BF),
    "b": ((D, L), BF),
    "rstd": ((16, L), F32),
}
BACK = {
    "gs": ((len(UNITS), S, 2 * S), BF),
    "gz": ((D, L), BF),
    "gy": ((D, L), BF),
    "gh": ((FF, L), BF),
    "gpk": ((3 * D, L), BF),
}
RAW = ("gains", "shifts", "hidden", "wi", "wo", "m1", "m2")
PREP = {
    "cols": ((6, D, S), F32),
    "hid": ((FF, S), F32),
    "wi_t": ((3 * D, D), BF),
    "wo_t": ((D, D), BF),
    "m1_t": ((FF, D), BF),
    "m2_t": ((D, FF), BF),
    "m2_h": ((FF, D), BF),
}


def spread_row(row):
    return jnp.transpose(jnp.broadcast_to(row, (S, D)))


def prep_weights(l, raw, prep, forward):
    raw = dict(zip(RAW, raw))
    prep = dict(zip(PREP, prep))

    @pl.when(pl.program_id(0) == 0)
    def _():
        for j in range(2):
            prep["cols"][j] = spread_row(raw["gains"][l, j:j + 1, :])
        for j in range(4):
            prep["cols"][2 + j] = spread_row(raw["shifts"][l, j:j + 1, :])
        if forward:
            for j in range(4):
                rows = slice(j * D, (j + 1) * D)
                prep["hid"][rows, :] = spread_row(raw["hidden"][l:l + 1, rows])
                prep["m1_t"][rows, :] = jnp.transpose(raw["m1"][l, :, rows])
                prep["m2_t"][:, rows] = jnp.transpose(raw["m2"][l, rows, :]) * BF(0.5)
            for j in range(3):
                rows = slice(j * D, (j + 1) * D)
                prep["wi_t"][rows, :] = jnp.transpose(raw["wi"][l, :, rows])
            prep["wo_t"][...] = jnp.transpose(raw["wo"][l])
        prep["m2_h"][...] = raw["m2"][l] * BF(0.5)

    return prep | {name: raw[name].at[l] for name in ("wi", "wo", "m1")}


def scratch_of(table, ng):
    return [pltpu.VMEM((ng,) + shape, dt) for shape, dt in table.values()]


def prep_scratch():
    return [pltpu.VMEM(shape, dt) for shape, dt in PREP.values()]


def views(names, refs, g):
    return {name: ref.at[g] for name, ref in zip(names, refs)}


def sharing(group_views, per_turn, view_at, bias_at):
    return {
        "per_turn": per_turn,
        "views": group_views,
        "last": group_views[-1],
        "low": None,
        "high": None,
        "redo": lambda low, high: redo_shifted(low, high, view_at, bias_at, len(group_views)),
    }


def encode_kernel(x_ref, seg_ref, vis_ref, *rest):
    raw, rest = rest[:len(RAW)], rest[len(RAW):]
    enc_ref = rest[0]
    saved = rest[1:1 + len(SAVED)]
    w = prep_weights(0, raw, rest[1 + len(SAVED):], True)
    share = sharing([views(SAVED, saved, g) for g in range(NG_E)], TURN_E, lambda g: views(SAVED, saved, g),
                    lambda g: masks(seg_ref, vis_ref, NT * g, False))

    def group(g):
        sv = share["views"][g]
        bias = masks(seg_ref, vis_ref, NT * g, False)
        x = jnp.concatenate([jnp.transpose(x_ref[NT * g + t]).astype(F32) for t in range(NT)], axis=1)
        yield
        out = yield from layer_fwd(x, bias, w, sv, share)
        enc_ref[g] = out.astype(BF)

    drive([group(g) for g in range(NG_E)])


def zero_first(refs):
    @pl.when(pl.program_id(0) == 0)
    def _():
        for ref in refs:
            ref[...] = jnp.zeros_like(ref)


ACC = [
    ((4, D, S), F32),
    ((3 * D, D), F32),
    ((D + HEAD, D), F32),
    ((FF, 2 * D), F32),
    ((FF + HEAD, D), F32),
]


def finish(acc, out, a_mask=None):
    a_vec, a_wi, a_wo, a_m1, a_m2 = acc

    @pl.when(pl.program_id(0) == pl.num_programs(0) - 1)
    def _():
        out[0:FF, :] = a_m2[0:FF, :] * 0.5
        for j in range(4):
            rows = slice(j * D, (j + 1) * D)
            out[FF + j * D:FF + (j + 1) * D, :] = jnp.transpose(a_m1[rows, 0:D])
            out[SMALL + 6 + j:SMALL + 7 + j, :] = jnp.transpose(a_m1[rows, D:2 * D])[0:1]
            out[SMALL + j:SMALL + j + 1, :] = jnp.sum(jnp.transpose(a_vec[j]), axis=0, keepdims=True)
        for j in range(3):
            rows = slice(j * D, (j + 1) * D)
            out[2 * FF + j * D:2 * FF + (j + 1) * D, :] = jnp.transpose(a_wi[rows, :])
        out[2 * FF + 3 * D:SMALL, :] = a_wo[0:D, :]
        out[SMALL + 4:SMALL + 5, :] = a_wo[D:D + 1, :]
        out[SMALL + 5:SMALL + 6, :] = a_m2[FF:FF + 1, :]
        out[SMALL + 11:PACKED, :] = jnp.zeros((PACKED - SMALL - 11, D), F32)
        out[SMALL + 10:SMALL + 11, :] = jnp.zeros((1, D), F32)
        if a_mask is not None:
            out[SMALL + 10:SMALL + 11, :] = jnp.sum(jnp.transpose(a_mask[...]), axis=0, keepdims=True)


def decode_kernel(inv_order, enc_ref, *rest):
    cots = rest[:(NT * NG_D)]
    seg_ref, vis_ref, mask_row = rest[(NT * NG_D):(NT * NG_D) + 3]
    rest = rest[(NT * NG_D) + 3:]
    raw, rest = rest[:len(RAW)], rest[len(RAW):]
    dec_out, ge_ref, out_ref = rest[:3]
    rest = rest[3:]
    acc, rest = rest[:len(ACC)], rest[len(ACC):]
    a_mask, maskcol, dec_ref, sems = rest[:4]
    rest = rest[4:]
    w = prep_weights(1, raw, rest[:len(PREP)], True)
    scr = rest[len(PREP):]
    step = pl.program_id(0)
    slot = lax.rem(step, 2)

    @pl.when(step == 0)
    def _():
        maskcol[...] = spread_row(mask_row[0:1, :])

    def copies(at, where):
        return [
            pltpu.make_async_copy(dec_ref.at[where, t], dec_out.at[inv_order[(NT * NG_D) * at + t]], sems.at[where, t])
            for t in range((NT * NG_D))
        ]

    @pl.when(step >= 2)
    def _():
        for copy in copies(step - 2, slot):
            copy.wait()

    zero_first(acc + (a_mask,))
    table = list(SAVED) + list(BACK)
    share = sharing([views(table, scr, g) for g in range(NG_D)], TURN_D, lambda g: views(table, scr, g),
                    lambda g: masks(seg_ref, vis_ref, NT * g, True))

    def group(g):
        sv = share["views"][g]
        bias = masks(seg_ref, vis_ref, NT * g, True)
        shown = jnp.concatenate([vis_ref[0, NT * g + t:NT * g + t + 1, :] for t in range(NT)], axis=1) == 1
        x = jnp.where(shown, enc_ref[g].astype(F32), wide(maskcol[...]))
        yield
        out = yield from layer_fwd(x, bias, w, sv, share)
        outb = out.astype(BF)
        for t in range(NT):
            dec_ref[slot, NT * g + t] = jnp.transpose(outb[:, t * S:(t + 1) * S])
        yield
        grad = jnp.concatenate([jnp.transpose(cots[NT * g + t][0]).astype(F32) for t in range(NT)], axis=1)
        yield
        grad = yield from layer_bwd(grad, w, sv, acc, share)
        a_mask[...] += fold(jnp.where(shown, 0.0, grad))
        ge_ref[g] = jnp.where(shown, grad, 0.0).astype(BF)

    drive([group(g) for g in range(NG_D)])
    for copy in copies(step, slot):
        copy.start()

    @pl.when(step == pl.num_programs(0) - 1)
    def _():
        for copy in copies(step - 1, 1 - slot) + copies(step, slot):
            copy.wait()

    finish(acc, out_ref, a_mask)


def back_kernel(core_ref, ge_ref, other_ref, *rest):
    saved = rest[:len(SAVED)]
    rest = rest[len(SAVED):]
    raw, rest = rest[:len(RAW)], rest[len(RAW):]
    tg_ref, keep_ref, send_ref = rest[:3]
    out_ref, rest = rest[3], rest[4:]
    acc, rest = rest[:len(ACC)], rest[len(ACC):]
    w = prep_weights(0, raw, rest[:len(PREP)], False)
    scr = rest[len(PREP):]
    zero_first(acc)
    share = sharing([views(SAVED, saved, g) | views(BACK, scr, g) for g in range(NG_B)], TURN_B, None, None)

    def group(g):
        sv = share["views"][g]
        grad = ge_ref[g].astype(F32)
        yield
        grad = yield from layer_bwd(grad, w, sv, acc, share)
        for t in range(NT):
            tg_ref[NT * g + t] = jnp.transpose(grad[:, t * S:(t + 1) * S])

    drive([group(g) for g in range(NG_B)])
    finish(acc, out_ref)

    @pl.when((pl.program_id(0) == pl.num_programs(0) - 1) & (core_ref[0] == 0))
    def _():
        keep_ref[...] = out_ref[...]
        send_ref[...] = other_ref[...].astype(BF)

    @pl.when((pl.program_id(0) == pl.num_programs(0) - 1) & (core_ref[0] == 1))
    def _():
        keep_ref[...] = other_ref[...]
        send_ref[...] = out_ref[...].astype(BF)


def const_spec(arr):
    return pl.BlockSpec(arr.shape, lambda *_: (0,) * arr.ndim)


def step_spec(shape):
    return pl.BlockSpec(shape, lambda i, *_: (i,) + (0,) * (len(shape) - 1))


PARAMS = pltpu.CompilerParams(dimension_semantics=("arbitrary",), vmem_limit_bytes=60 * 1024 * 1024)
GRADS = [jax.ShapeDtypeStruct((PACKED, D), F32)]


def cost(flops, nbytes):
    return pl.CostEstimate(flops=flops, bytes_accessed=nbytes, transcendentals=0)


def run_encode(x, seg, vis, w):
    tiles = x.shape[0]
    groups, steps = tiles // NT, tiles // (NT * NG_E)
    ops = list(w)
    out_shape = [jax.ShapeDtypeStruct((groups, D, L), BF)]
    out_shape += [jax.ShapeDtypeStruct((groups,) + shape, dt) for shape, dt in SAVED.values()]
    return pl.pallas_call(
        encode_kernel,
        grid=(steps,),
        in_specs=[step_spec(((NT * NG_E), S, D)), step_spec((1, (NT * NG_E), S)), step_spec((1, (NT * NG_E), S))] + [const_spec(o) for o in ops],
        out_specs=[step_spec((NG_E,) + o.shape[1:]) for o in out_shape],
        out_shape=out_shape,
        scratch_shapes=prep_scratch(),
        cost_estimate=cost(20 * 10**9, 60 * 10**6),
        compiler_params=PARAMS,
    )(x, seg.reshape(steps, (NT * NG_E), S), vis.reshape(steps, (NT * NG_E), S), *ops)


def run_decode(inv_order, enc, cot, seg, vis, mask_row, w):
    tiles = cot.shape[0]
    groups, steps = tiles // NT, tiles // (NT * NG_D)
    ops = [mask_row] + list(w)
    cot_specs = [pl.BlockSpec((1, S, D), lambda i, o, t=t: (o[(NT * NG_D) * i + t], 0, 0)) for t in range((NT * NG_D))]
    out_shape = [jax.ShapeDtypeStruct((tiles, S, D), BF), jax.ShapeDtypeStruct((groups, D, L), BF)] + GRADS
    return pl.pallas_call(
        decode_kernel,
        grid_spec=pltpu.PrefetchScalarGridSpec(
            num_scalar_prefetch=1,
            grid=(steps,),
            in_specs=[step_spec((NG_D, D, L))] + cot_specs + [step_spec((1, (NT * NG_D), S))] * 2 + [const_spec(o) for o in ops],
            out_specs=[pl.BlockSpec(memory_space=pl.ANY), step_spec((NG_D, D, L))] + [const_spec(o) for o in GRADS],
            scratch_shapes=[pltpu.VMEM(shape, dt) for shape, dt in ACC] + [pltpu.VMEM((D, S), F32)] * 2
            + [pltpu.VMEM((2, (NT * NG_D), S, D), BF), pltpu.SemaphoreType.DMA((2, (NT * NG_D)))]
            + prep_scratch() + scratch_of(SAVED, NG_D) + scratch_of(BACK, NG_D),
        ),
        out_shape=out_shape,
        cost_estimate=cost(40 * 10**9, 10 * 10**6),
        compiler_params=PARAMS,
    )(inv_order, enc, *([cot] * (NT * NG_D)), seg.reshape(steps, (NT * NG_D), S), vis.reshape(steps, (NT * NG_D), S), *ops)


def run_back(core, ge, other, saved, w):
    groups = ge.shape[0]
    steps = groups // NG_B
    ops = list(w)
    packed = jax.ShapeDtypeStruct((PACKED, D), F32)
    out_shape = [jax.ShapeDtypeStruct((groups * NT, S, D), F32), packed, jax.ShapeDtypeStruct((PACKED, D), BF)]
    return pl.pallas_call(
        back_kernel,
        grid_spec=pltpu.PrefetchScalarGridSpec(
            num_scalar_prefetch=1,
            grid=(steps,),
            in_specs=[step_spec((NG_B, D, L)), const_spec(other)] + [step_spec((NG_B,) + v.shape[1:]) for v in saved]
            + [const_spec(o) for o in ops],
            out_specs=[step_spec((NT * NG_B, S, D))] + [const_spec(o) for o in out_shape[1:]],
            scratch_shapes=[pltpu.VMEM((PACKED, D), F32)] + [pltpu.VMEM(shape, dt) for shape, dt in ACC] + prep_scratch()
            + scratch_of(BACK, NG_B),
        ),
        out_shape=out_shape,
        compiler_params=PARAMS,
        cost_estimate=cost(20 * 10**9, 60 * 10**6),
    )(core, ge, other, *saved, *ops)


def unpack_kernel(core_ref, mine, other, g_m2, g_m1, g_wi, g_wo, g_gain, g_shift, g_hid, g_mask):
    core = core_ref[0]

    def write(src, l):
        g_m2[l] = src[0:FF, :].astype(F32)
        for j in range(4):
            g_m1[l, :, j * D:(j + 1) * D] = src[FF + j * D:FF + (j + 1) * D, :].astype(F32)
        for j in range(3):
            g_wi[l, :, j * D:(j + 1) * D] = src[2 * FF + j * D:2 * FF + (j + 1) * D, :].astype(F32)
        g_wo[l] = src[2 * FF + 3 * D:SMALL, :].astype(F32)
        rows = src[SMALL:SMALL + 16, :].astype(F32)
        g_gain[l] = rows[0:2]
        g_shift[l] = rows[2:6]
        for j in range(4):
            g_hid[l:l + 1, j * D:(j + 1) * D] = rows[6 + j:7 + j]
        if l == 1:
            g_mask[...] = rows[10:11]

    @pl.when(core == 0)
    def _():
        write(mine, 0)
        write(other, 1)

    @pl.when(core == 1)
    def _():
        write(other, 0)
        write(mine, 1)


def unpack(core, mine, other):
    shapes = [(2, FF, D), (2, D, FF), (2, D, 3 * D), (2, D, D), (2, 2, D), (2, 4, D), (2, FF), (1, D)]
    return pl.pallas_call(
        unpack_kernel,
        grid_spec=pltpu.PrefetchScalarGridSpec(
            num_scalar_prefetch=1,
            grid=(1,),
            in_specs=[const_spec(mine), const_spec(other)],
            out_specs=[pl.BlockSpec(sh, lambda *_, n=len(sh): (0,) * n) for sh in shapes],
        ),
        out_shape=[jax.ShapeDtypeStruct(sh, F32) for sh in shapes],
        compiler_params=PARAMS,
    )(core.reshape(1).astype(jnp.int32), mine, other)


def swap(value, axis, bits, size):
    return lax.ppermute(value, axis, [(i, i ^ bits) for i in range(size)])


def split(value, bit):
    half = value.shape[0] // 2
    keep = lax.dynamic_slice_in_dim(value, bit * half, half, axis=0)
    send = lax.dynamic_slice_in_dim(value, (1 - bit) * half, half, axis=0)
    return keep, send.astype(BF)


def join(mine, other, bit):
    return jnp.where(bit == 0, jnp.concatenate([mine, other], axis=0), jnp.concatenate([other, mine], axis=0))


def reduce_all(keep, send, n_dp, n_group):
    x = lax.axis_index("group")
    value = keep + swap(send, "dp", 1, n_dp).astype(F32)
    for bits, bit in ((3, x // 2), (1, x % 2)):
        keep, send = split(value, bit)
        value = keep + swap(send, "group", bits, n_group).astype(F32)
    for bits in (2, 6, 8, 24):
        value = value + swap(value.astype(BF), "dp", bits, n_dp).astype(F32)
    value = value.astype(BF)
    for bits, bit in ((1, x % 2), (3, x // 2)):
        value = join(value, swap(value, "group", bits, n_group), bit)
    other = swap(value, "dp", 1, n_dp)
    return value, other


def on_device(token_tiles, segment_ids, visible_flags, tile_order, mask_token, norm_gains, shift_terms,
              attn_in, attn_out, mlp_in, hidden_shift, mlp_out, cotangent):
    tiles = token_tiles.shape[2]
    full_shape = (1, 1, tiles, S, D)
    order = tile_order.reshape(tiles)
    spots = jnp.arange(tiles, dtype=jnp.int32)
    inv_order = jnp.sum(jnp.where(order[None, :] == spots[:, None], spots[None, :], 0), axis=1).astype(jnp.int32)
    cot = lax.all_to_all(cotangent.reshape(tiles, S, D), "dp", split_axis=0, concat_axis=0, tiled=True)
    w = (norm_gains, shift_terms, hidden_shift, attn_in, attn_out, mlp_in, mlp_out)
    seg, vis = segment_ids.reshape(tiles, S), visible_flags.reshape(tiles, S)
    enc, *saved = run_encode(token_tiles.reshape(tiles, S, D), seg, vis, w)
    dec, ge, packed1 = run_decode(inv_order, enc, cot, seg, vis, mask_token.reshape(1, D), w)
    decoded = lax.all_to_all(dec, "dp", split_axis=0, concat_axis=0, tiled=True)
    core = lax.rem(lax.axis_index("dp"), 2).astype(jnp.int32)
    tg, keep, send = run_back(core.reshape(1), ge, packed1, saved, w)
    n_dp = lax.axis_size("dp")
    if n_dp == 32:
        decoded, send = lax.optimization_barrier((decoded, send))
        mine, other = reduce_all(keep, send, n_dp, lax.axis_size("group"))
    else:
        mine, other = keep.astype(BF), send
    g_m2, g_m1, g_wi, g_wo, g_gain, g_shift, g_hid, g_mask = unpack(core, mine, other)
    return (
        decoded.reshape(full_shape),
        tg.reshape(full_shape),
        g_mask.reshape(D),
        g_gain,
        g_shift,
        g_wi,
        g_wo,
        g_m1,
        g_hid,
        g_m2,
    )


def solution(mesh):
    tile5 = P("dp", "group", None, None, None)
    in_specs = (tile5, P("dp", "group", None, None), P("dp", "group", None, None), P("dp", "group", None),
                P(), P(), P(), P(), P(), P(), P(), P(), tile5)
    out_specs = (tile5, tile5) + (P(),) * 8
    return jax.shard_map(on_device, mesh=mesh, in_specs=in_specs, out_specs=out_specs, check_vma=False)
```

```python
import jax
import jax.numpy as jnp
from jax import lax
from jax.experimental import pallas as pl
from jax.experimental.pallas import tpu as pltpu
from jax.sharding import PartitionSpec as P

HEADS = 8
HEAD = 16
D = 128
FF = 512
S = 128
NT = 2
NG_E = 8
TURN_E = 2
TURN_D = 2
TURN_B = 2
NG_D = 8
NG_B = 4
L = NT * S
SMALL = 2 * FF + 4 * D
PACKED = SMALL + 64
EPS = 1e-5
LOG2E = 1.4426950408889634
LN2 = 0.6931471805599453
F32 = jnp.float32
BF = jnp.bfloat16


def nn(a, b):
    return lax.dot_general(a, b, (((1,), (0,)), ((), ())), preferred_element_type=F32)


def nt(a, b):
    return lax.dot_general(a, b, (((1,), (1,)), ((), ())), preferred_element_type=F32)


def wide(col):
    return jnp.concatenate([col] * NT, axis=1)


def fold(val):
    out = val[:, :S]
    for t in range(1, NT):
        out = out + val[:, t * S:(t + 1) * S]
    return out


def normalize(x):
    center = x - jnp.sum(x, axis=0, keepdims=True) * (1.0 / D)
    var = jnp.sum(center * center, axis=0, keepdims=True) * (1.0 / D)
    rstd = lax.rsqrt(var + EPS)
    return center * rstd, rstd


def norm_back(grad, xhat, rstd, gain):
    gx = grad * gain
    m1 = jnp.sum(gx, axis=0, keepdims=True) * (1.0 / D)
    m2 = jnp.sum(gx * xhat, axis=0, keepdims=True) * (1.0 / D)
    return (gx - m1 - xhat * m2) * rstd


def padded(rows, h):
    parts = []
    if h > 0:
        parts.append(jnp.zeros((HEAD * h, S), BF))
    parts.append(rows)
    if h < HEADS - 1:
        parts.append(jnp.zeros((D - HEAD * (h + 1), S), BF))
    return jnp.concatenate(parts, axis=0)


def pair_rhs(two, h):
    return jnp.concatenate([padded(two[0:HEAD], h), padded(two[HEAD:2 * HEAD], h + 1)], axis=1)


def flip_pair(two):
    return jnp.concatenate([jnp.transpose(two[:, 0:S]), jnp.transpose(two[:, S:2 * S])], axis=1)


def quad_lhs(one, two):
    zero = jnp.zeros_like(one)
    return jnp.concatenate(
        [jnp.concatenate([one, zero], axis=1), jnp.concatenate([zero, two], axis=1)], axis=0)


def pair_lhs(two):
    zero = jnp.zeros((HEAD, S), BF)
    return jnp.concatenate(
        [jnp.concatenate([two[0:HEAD], zero], axis=1), jnp.concatenate([zero, two[HEAD:2 * HEAD]], axis=1)], axis=0)


UNITS = [(t, h) for t in range(NT) for h in range(0, HEADS, 2)]


def mix_values(sv, t, h):
    sl = slice(t * S, (t + 1) * S)
    v = [sv["p"][2 * D + HEAD * (h + 2 * q):2 * D + HEAD * (h + 2 * q + 2), sl] for q in range(2)]
    ones = jnp.ones((HEAD // 2, S), BF)
    left = jnp.concatenate([quad_lhs(*v), quad_lhs(ones, ones)], axis=0)
    o = nn(left, jnp.concatenate([sv["e"][t, :, (h + 2 * q) * S:(h + 2 * q + 2) * S] for q in range(2)], axis=0))
    totals = []
    for k in range(4):
        kl = slice(k % 2 * S, (k % 2 + 1) * S)
        totals.append(o[4 * HEAD + 8 * (k // 2):4 * HEAD + 8 * (k // 2) + 8, kl])
        inv = 1.0 / totals[k]
        sv["inv"][8 * (h + k):8 * (h + k) + 8, sl] = inv
        sv["o"][HEAD * (h + k):HEAD * (h + k + 1), sl] = (
            o[HEAD * k:HEAD * (k + 1), kl] * jnp.concatenate([inv, inv], axis=0)).astype(BF)
    return totals


def redo_shifted(low, high, group_view, group_bias, ng):
    safe = (jnp.min(low) > 2.0 ** -60) & (jnp.max(high) < 2.0 ** 60)

    @pl.when(jnp.logical_not(safe))
    def _():
        def one(g, carry):
            sv = group_view(g)
            biases = group_bias(g)
            for t, h in UNITS:
                sl = slice(t * S, (t + 1) * S)
                keys = jnp.transpose(sv["p"][D:2 * D, sl])
                scores = nn(keys, pair_rhs(sv["p"][HEAD * h:HEAD * (h + 2), sl], h))
                for k in range(2):
                    part = scores[:, k * S:(k + 1) * S] + biases[t]
                    e = jnp.exp2(part - jnp.max(part, axis=0, keepdims=True))
                    sv["e"][t, :, (h + k) * S:(h + k + 1) * S] = e.astype(BF)
                if h % 4:
                    mix_values(sv, t, h - 2)
            return carry

        lax.fori_loop(0, ng, one, 0)


def layer_fwd(x, biases, w, sv, share):
    per_turn = share["per_turn"]
    wi_t, wo_t, m1_t, m2_t, cols, hid = w["wi_t"], w["wo_t"], w["m1_t"], w["m2_t"], w["cols"], w["hid"]
    xhat0, rstd0 = normalize(x)
    sv["xhat0"][...] = xhat0.astype(BF)
    sv["rstd"][0:8, :] = jnp.broadcast_to(rstd0, (8, L))
    a = (xhat0 * wide(cols[0]) + wide(cols[2])).astype(BF)
    sv["a"][...] = a
    p = nn(wi_t[...], a)
    yield
    sv["p"][0:D, :] = (p[0:D] * (0.25 * LOG2E)).astype(BF)
    sv["p"][D:3 * D, :] = p[D:3 * D].astype(BF)
    yield
    keys = [jnp.transpose(sv["p"][D:2 * D, t * S:(t + 1) * S]) for t in range(NT)]
    n = len(UNITS)
    for turn in range(0, n + per_turn, per_turn):
        for t, h in UNITS[turn:turn + per_turn]:
            scores = nn(keys[t], pair_rhs(sv["p"][HEAD * h:HEAD * (h + 2), t * S:(t + 1) * S], h))
            for k in range(2):
                e = jnp.exp2(scores[:, k * S:(k + 1) * S] + biases[t])
                sv["e"][t, :, (h + k) * S:(h + k + 1) * S] = e.astype(BF)
        for t, h in UNITS[max(turn - per_turn, 0):turn:2]:
            for total in mix_values(sv, t, h):
                share["low"] = total if share["low"] is None else jnp.minimum(share["low"], total)
                share["high"] = total if share["high"] is None else jnp.maximum(share["high"], total)
        yield
    if share["last"] is sv:
        share["redo"](share["low"], share["high"])
    yield
    x1 = x + nn(wo_t[...], sv["o"][...]) + wide(cols[4])
    yield
    xhat1, rstd1 = normalize(x1)
    sv["xhat1"][...] = xhat1.astype(BF)
    sv["rstd"][8:16, :] = jnp.broadcast_to(rstd1, (8, L))
    b = (xhat1 * wide(cols[1]) + wide(cols[3])).astype(BF)
    sv["b"][...] = b
    yield
    hidden = None
    for i in range(5):
        last = hidden
        if i < 4:
            hidden = nn(m1_t[i * D:(i + 1) * D, :], b)
        if i >= 1:
            rows = slice((i - 1) * D, i * D)
            hv = last + wide(hid[rows, :])
            arg = hv * 0.7071067811865476
            cdf2 = lax.erf(arg) + 1.0
            sv["u"][rows, :] = (hv * cdf2).astype(BF)
            bell = jnp.exp2(arg * arg * -LOG2E)
            sv["gp"][rows, :] = (cdf2 + arg * 1.1283791670955126 * bell).astype(BF)
        yield
    return x1 + nn(m2_t[...], sv["u"][...]) + wide(cols[5])


def lanes(views, name):
    return jnp.concatenate([sv[name][...] for sv in views], axis=1)


def layer_bwd(g2, w, sv, acc, share):
    wi, wo, m1, m2, cols = w["wi"], w["wo"], w["m1"], w["m2_h"], w["cols"]
    a_vec, a_wi, a_wo, a_m1, a_m2 = acc
    views = share["views"]
    per_turn = share["per_turn"]
    last = views[-1] is sv
    n = len(UNITS)
    gz = g2.astype(BF)
    sv["gz"][...] = gz
    gu = None
    for i in range(3):
        done = gu
        if i < 2:
            gu = nn(m2[i * 2 * D:(i + 1) * 2 * D, :], gz)
        if i >= 1:
            rows = slice((i - 1) * 2 * D, i * 2 * D)
            sv["gh"][rows, :] = (done * sv["gp"][rows, :].astype(F32)).astype(BF)
        yield
    gb = nn(m1[...], sv["gh"][...])
    yield
    if last:
        width = L * len(views)
        a_m2[...] += nt(jnp.concatenate([lanes(views, "u"), jnp.ones((HEAD, width), BF)], axis=0), lanes(views, "gz"))
    yield
    if last:
        a_m1[...] += nt(lanes(views, "gh"), jnp.concatenate([lanes(views, "b"), jnp.ones((D, width), BF)], axis=0))
    yield
    xhat1 = sv["xhat1"][...].astype(F32)
    a_vec[1] += fold(gb * xhat1)
    a_vec[3] += fold(gb)
    g1 = g2 + norm_back(gb, xhat1, sv["rstd"][8:9, :], wide(cols[1]))
    gy = g1.astype(BF)
    sv["gy"][...] = gy
    yield
    go = nn(wo[...], gy)
    yield
    if last:
        a_wo[...] += nt(jnp.concatenate([lanes(views, "o"), jnp.ones((HEAD, width), BF)], axis=0), lanes(views, "gy"))
    values = [jnp.transpose(sv["p"][2 * D:3 * D, t * S:(t + 1) * S]) for t in range(NT)]
    gobs = {}
    for turn in range(0, n + per_turn, per_turn):
        for i in range(turn, min(turn + per_turn, n)):
            t, h = UNITS[i]
            sl = slice(t * S, (t + 1) * S)
            parts, rs = [], []
            for k in (h, h + 1):
                hs = slice(HEAD * k, HEAD * (k + 1))
                inv = sv["inv"][8 * k:8 * k + 8, sl]
                gob = (go[hs, sl] * jnp.concatenate([inv, inv], axis=0)).astype(BF)
                parts.append(gob)
                rs.append(jnp.sum(gob.astype(F32) * sv["o"][hs, sl].astype(F32), axis=0, keepdims=True))
            gobs[i] = jnp.concatenate(parts, axis=0)
            gf = nn(values[t], pair_rhs(gobs[i], h))
            for k in range(2):
                kl = slice(k * S, (k + 1) * S)
                e = sv["e"][t, :, (h + k) * S:(h + k + 1) * S].astype(F32)
                sv["gs"][i, :, kl] = (e * (gf[:, kl] - rs[k])).astype(BF)
        for i in range(max(turn - per_turn, 0), turn, 2):
            t, h = UNITS[i]
            sl = slice(t * S, (t + 1) * S)
            gs2 = [sv["gs"][i], sv["gs"][i + 1]]
            e2 = [sv["e"][t, :, (h + 2 * q) * S:(h + 2 * q + 2) * S] for q in range(2)]
            pv = nn(quad_lhs(gobs[i], gobs[i + 1]), jnp.concatenate([flip_pair(v) for v in e2], axis=0))
            pq = nn(quad_lhs(*[sv["p"][D + HEAD * (h + 2 * q):D + HEAD * (h + 2 * q + 2), sl] for q in range(2)]),
                    jnp.concatenate(gs2, axis=0))
            pk = nn(quad_lhs(*[sv["p"][HEAD * (h + 2 * q):HEAD * (h + 2 * q + 2), sl] for q in range(2)]),
                    jnp.concatenate([flip_pair(v) for v in gs2], axis=0))
            for k in range(4):
                kr = slice(HEAD * k, HEAD * (k + 1))
                kl = slice(k % 2 * S, (k % 2 + 1) * S)
                at = HEAD * (h + k)
                sv["gpk"][at:at + HEAD, sl] = (pq[kr, kl] * 0.25).astype(BF)
                sv["gpk"][D + at:D + at + HEAD, sl] = (pk[kr, kl] * LN2).astype(BF)
                sv["gpk"][2 * D + at:2 * D + at + HEAD, sl] = pv[kr, kl].astype(BF)
        yield
    ga = nn(wi[...], sv["gpk"][...])
    yield
    if last:
        a_wi[...] += nt(lanes(views, "gpk"), lanes(views, "a"))
    xhat0 = sv["xhat0"][...].astype(F32)
    a_vec[0] += fold(ga * xhat0)
    a_vec[2] += fold(ga)
    return g1 + norm_back(ga, xhat0, sv["rstd"][0:1, :], wide(cols[0]))


def masks(seg_ref, vis_ref, first, decoder):
    rows_i = lax.broadcasted_iota(jnp.int32, (S, S), 0)
    cols_i = lax.broadcasted_iota(jnp.int32, (S, S), 1)
    diag = rows_i == cols_i
    out = []
    for t in range(NT):
        seg = seg_ref[0, pl.ds(first + t, 1), :]
        key = jnp.where(seg >= 0, seg, -2)
        if not decoder:
            key = jnp.where(vis_ref[0, pl.ds(first + t, 1), :] == 1, key, -2)
        key_k = jnp.transpose(jnp.broadcast_to(key, (S, S)).astype(F32))
        out.append(jnp.where((key_k == seg.astype(F32)) | diag, 0.0, -1e30))
    return out


def drive(gens):
    gens = list(gens)
    while gens:
        alive = []
        for gen in gens:
            try:
                next(gen)
                alive.append(gen)
            except StopIteration:
                pass
        gens = alive


SAVED = {
    "p": ((3 * D, L), BF),
    "e": ((NT, S, HEADS * S), BF),
    "inv": ((8 * HEADS, L), F32),
    "o": ((D, L), BF),
    "u": ((FF, L), BF),
    "gp": ((FF, L), BF),
    "xhat0": ((D, L), BF),
    "xhat1": ((D, L), BF),
    "a": ((D, L), BF),
    "b": ((D, L), BF),
    "rstd": ((16, L), F32),
}
BACK = {
    "gs": ((len(UNITS), S, 2 * S), BF),
    "gz": ((D, L), BF),
    "gy": ((D, L), BF),
    "gh": ((FF, L), BF),
    "gpk": ((3 * D, L), BF),
}
RAW = ("gains", "shifts", "hidden", "wi", "wo", "m1", "m2")
PREP = {
    "cols": ((6, D, S), F32),
    "hid": ((FF, S), F32),
    "wi_t": ((3 * D, D), BF),
    "wo_t": ((D, D), BF),
    "m1_t": ((FF, D), BF),
    "m2_t": ((D, FF), BF),
    "m2_h": ((FF, D), BF),
}


def spread_row(row):
    return jnp.transpose(jnp.broadcast_to(row, (S, D)))


def prep_weights(l, raw, prep, forward):
    raw = dict(zip(RAW, raw))
    prep = dict(zip(PREP, prep))

    @pl.when(pl.program_id(0) == 0)
    def _():
        for j in range(2):
            prep["cols"][j] = spread_row(raw["gains"][l, j:j + 1, :])
        for j in range(4):
            prep["cols"][2 + j] = spread_row(raw["shifts"][l, j:j + 1, :])
        if forward:
            for j in range(4):
                rows = slice(j * D, (j + 1) * D)
                prep["hid"][rows, :] = spread_row(raw["hidden"][l:l + 1, rows])
                prep["m1_t"][rows, :] = jnp.transpose(raw["m1"][l, :, rows])
                prep["m2_t"][:, rows] = jnp.transpose(raw["m2"][l, rows, :]) * BF(0.5)
            for j in range(3):
                rows = slice(j * D, (j + 1) * D)
                prep["wi_t"][rows, :] = jnp.transpose(raw["wi"][l, :, rows])
            prep["wo_t"][...] = jnp.transpose(raw["wo"][l])
        prep["m2_h"][...] = raw["m2"][l] * BF(0.5)

    return prep | {name: raw[name].at[l] for name in ("wi", "wo", "m1")}


def scratch_of(table, ng):
    return [pltpu.VMEM((ng,) + shape, dt) for shape, dt in table.values()]


def prep_scratch():
    return [pltpu.VMEM(shape, dt) for shape, dt in PREP.values()]


def views(names, refs, g):
    return {name: ref.at[g] for name, ref in zip(names, refs)}


def sharing(group_views, per_turn, view_at, bias_at):
    return {
        "per_turn": per_turn,
        "views": group_views,
        "last": group_views[-1],
        "low": None,
        "high": None,
        "redo": lambda low, high: redo_shifted(low, high, view_at, bias_at, len(group_views)),
    }


def encode_kernel(x_ref, seg_ref, vis_ref, *rest):
    raw, rest = rest[:len(RAW)], rest[len(RAW):]
    enc_ref = rest[0]
    saved = rest[1:1 + len(SAVED)]
    w = prep_weights(0, raw, rest[1 + len(SAVED):], True)
    share = sharing([views(SAVED, saved, g) for g in range(NG_E)], TURN_E, lambda g: views(SAVED, saved, g),
                    lambda g: masks(seg_ref, vis_ref, NT * g, False))

    def group(g):
        sv = share["views"][g]
        bias = masks(seg_ref, vis_ref, NT * g, False)
        x = jnp.concatenate([jnp.transpose(x_ref[NT * g + t]).astype(F32) for t in range(NT)], axis=1)
        yield
        out = yield from layer_fwd(x, bias, w, sv, share)
        enc_ref[g] = out.astype(BF)

    drive([group(g) for g in range(NG_E)])


def zero_first(refs):
    @pl.when(pl.program_id(0) == 0)
    def _():
        for ref in refs:
            ref[...] = jnp.zeros_like(ref)


ACC = [
    ((4, D, S), F32),
    ((3 * D, D), F32),
    ((D + HEAD, D), F32),
    ((FF, 2 * D), F32),
    ((FF + HEAD, D), F32),
]


def finish(acc, out, a_mask=None):
    a_vec, a_wi, a_wo, a_m1, a_m2 = acc

    @pl.when(pl.program_id(0) == pl.num_programs(0) - 1)
    def _():
        out[0:FF, :] = a_m2[0:FF, :] * 0.5
        for j in range(4):
            rows = slice(j * D, (j + 1) * D)
            out[FF + j * D:FF + (j + 1) * D, :] = jnp.transpose(a_m1[rows, 0:D])
            out[SMALL + 6 + j:SMALL + 7 + j, :] = jnp.transpose(a_m1[rows, D:2 * D])[0:1]
            out[SMALL + j:SMALL + j + 1, :] = jnp.sum(jnp.transpose(a_vec[j]), axis=0, keepdims=True)
        for j in range(3):
            rows = slice(j * D, (j + 1) * D)
            out[2 * FF + j * D:2 * FF + (j + 1) * D, :] = jnp.transpose(a_wi[rows, :])
        out[2 * FF + 3 * D:SMALL, :] = a_wo[0:D, :]
        out[SMALL + 4:SMALL + 5, :] = a_wo[D:D + 1, :]
        out[SMALL + 5:SMALL + 6, :] = a_m2[FF:FF + 1, :]
        out[SMALL + 11:PACKED, :] = jnp.zeros((PACKED - SMALL - 11, D), F32)
        out[SMALL + 10:SMALL + 11, :] = jnp.zeros((1, D), F32)
        if a_mask is not None:
            out[SMALL + 10:SMALL + 11, :] = jnp.sum(jnp.transpose(a_mask[...]), axis=0, keepdims=True)


def decode_kernel(inv_order, enc_ref, *rest):
    cots = rest[:(NT * NG_D)]
    seg_ref, vis_ref, mask_row = rest[(NT * NG_D):(NT * NG_D) + 3]
    rest = rest[(NT * NG_D) + 3:]
    raw, rest = rest[:len(RAW)], rest[len(RAW):]
    dec_out, ge_ref, out_ref = rest[:3]
    rest = rest[3:]
    acc, rest = rest[:len(ACC)], rest[len(ACC):]
    a_mask, maskcol, dec_ref, sems = rest[:4]
    rest = rest[4:]
    w = prep_weights(1, raw, rest[:len(PREP)], True)
    scr = rest[len(PREP):]
    step = pl.program_id(0)
    slot = lax.rem(step, 2)

    @pl.when(step == 0)
    def _():
        maskcol[...] = spread_row(mask_row[0:1, :])

    def copies(at, where):
        return [
            pltpu.make_async_copy(dec_ref.at[where, t], dec_out.at[inv_order[(NT * NG_D) * at + t]], sems.at[where, t])
            for t in range((NT * NG_D))
        ]

    @pl.when(step >= 2)
    def _():
        for copy in copies(step - 2, slot):
            copy.wait()

    zero_first(acc + (a_mask,))
    table = list(SAVED) + list(BACK)
    share = sharing([views(table, scr, g) for g in range(NG_D)], TURN_D, lambda g: views(table, scr, g),
                    lambda g: masks(seg_ref, vis_ref, NT * g, True))

    def group(g):
        sv = share["views"][g]
        bias = masks(seg_ref, vis_ref, NT * g, True)
        shown = jnp.concatenate([vis_ref[0, NT * g + t:NT * g + t + 1, :] for t in range(NT)], axis=1) == 1
        x = jnp.where(shown, enc_ref[g].astype(F32), wide(maskcol[...]))
        yield
        out = yield from layer_fwd(x, bias, w, sv, share)
        outb = out.astype(BF)
        for t in range(NT):
            dec_ref[slot, NT * g + t] = jnp.transpose(outb[:, t * S:(t + 1) * S])
        yield
        grad = jnp.concatenate([jnp.transpose(cots[NT * g + t][0]).astype(F32) for t in range(NT)], axis=1)
        yield
        grad = yield from layer_bwd(grad, w, sv, acc, share)
        a_mask[...] += fold(jnp.where(shown, 0.0, grad))
        ge_ref[g] = jnp.where(shown, grad, 0.0).astype(BF)

    drive([group(g) for g in range(NG_D)])
    for copy in copies(step, slot):
        copy.start()

    @pl.when(step == pl.num_programs(0) - 1)
    def _():
        for copy in copies(step - 1, 1 - slot) + copies(step, slot):
            copy.wait()

    finish(acc, out_ref, a_mask)


def back_kernel(core_ref, ge_ref, other_ref, *rest):
    saved = rest[:len(SAVED)]
    rest = rest[len(SAVED):]
    raw, rest = rest[:len(RAW)], rest[len(RAW):]
    tg_ref, keep_ref, send_ref = rest[:3]
    out_ref, rest = rest[3], rest[4:]
    acc, rest = rest[:len(ACC)], rest[len(ACC):]
    w = prep_weights(0, raw, rest[:len(PREP)], False)
    scr = rest[len(PREP):]
    zero_first(acc)
    share = sharing([views(SAVED, saved, g) | views(BACK, scr, g) for g in range(NG_B)], TURN_B, None, None)

    def group(g):
        sv = share["views"][g]
        grad = ge_ref[g].astype(F32)
        yield
        grad = yield from layer_bwd(grad, w, sv, acc, share)
        for t in range(NT):
            tg_ref[NT * g + t] = jnp.transpose(grad[:, t * S:(t + 1) * S])

    drive([group(g) for g in range(NG_B)])
    finish(acc, out_ref)

    @pl.when((pl.program_id(0) == pl.num_programs(0) - 1) & (core_ref[0] == 0))
    def _():
        keep_ref[...] = out_ref[...]
        send_ref[...] = other_ref[...].astype(BF)

    @pl.when((pl.program_id(0) == pl.num_programs(0) - 1) & (core_ref[0] == 1))
    def _():
        keep_ref[...] = other_ref[...]
        send_ref[...] = out_ref[...].astype(BF)


def const_spec(arr):
    return pl.BlockSpec(arr.shape, lambda *_: (0,) * arr.ndim)


def step_spec(shape):
    return pl.BlockSpec(shape, lambda i, *_: (i,) + (0,) * (len(shape) - 1))


PARAMS = pltpu.CompilerParams(dimension_semantics=("arbitrary",), vmem_limit_bytes=60 * 1024 * 1024)
GRADS = [jax.ShapeDtypeStruct((PACKED, D), F32)]


def cost(flops, nbytes):
    return pl.CostEstimate(flops=flops, bytes_accessed=nbytes, transcendentals=0)


def run_encode(x, seg, vis, w):
    tiles = x.shape[0]
    groups, steps = tiles // NT, tiles // (NT * NG_E)
    ops = list(w)
    out_shape = [jax.ShapeDtypeStruct((groups, D, L), BF)]
    out_shape += [jax.ShapeDtypeStruct((groups,) + shape, dt) for shape, dt in SAVED.values()]
    return pl.pallas_call(
        encode_kernel,
        grid=(steps,),
        in_specs=[step_spec(((NT * NG_E), S, D)), step_spec((1, (NT * NG_E), S)), step_spec((1, (NT * NG_E), S))] + [const_spec(o) for o in ops],
        out_specs=[step_spec((NG_E,) + o.shape[1:]) for o in out_shape],
        out_shape=out_shape,
        scratch_shapes=prep_scratch(),
        cost_estimate=cost(20 * 10**9, 60 * 10**6),
        compiler_params=PARAMS,
    )(x, seg.reshape(steps, (NT * NG_E), S), vis.reshape(steps, (NT * NG_E), S), *ops)


def run_decode(inv_order, enc, cot, seg, vis, mask_row, w):
    tiles = cot.shape[0]
    groups, steps = tiles // NT, tiles // (NT * NG_D)
    ops = [mask_row] + list(w)
    cot_specs = [pl.BlockSpec((1, S, D), lambda i, o, t=t: (o[(NT * NG_D) * i + t], 0, 0)) for t in range((NT * NG_D))]
    out_shape = [jax.ShapeDtypeStruct((tiles, S, D), BF), jax.ShapeDtypeStruct((groups, D, L), BF)] + GRADS
    return pl.pallas_call(
        decode_kernel,
        grid_spec=pltpu.PrefetchScalarGridSpec(
            num_scalar_prefetch=1,
            grid=(steps,),
            in_specs=[step_spec((NG_D, D, L))] + cot_specs + [step_spec((1, (NT * NG_D), S))] * 2 + [const_spec(o) for o in ops],
            out_specs=[pl.BlockSpec(memory_space=pl.ANY), step_spec((NG_D, D, L))] + [const_spec(o) for o in GRADS],
            scratch_shapes=[pltpu.VMEM(shape, dt) for shape, dt in ACC] + [pltpu.VMEM((D, S), F32)] * 2
            + [pltpu.VMEM((2, (NT * NG_D), S, D), BF), pltpu.SemaphoreType.DMA((2, (NT * NG_D)))]
            + prep_scratch() + scratch_of(SAVED, NG_D) + scratch_of(BACK, NG_D),
        ),
        out_shape=out_shape,
        cost_estimate=cost(40 * 10**9, 10 * 10**6),
        compiler_params=PARAMS,
    )(inv_order, enc, *([cot] * (NT * NG_D)), seg.reshape(steps, (NT * NG_D), S), vis.reshape(steps, (NT * NG_D), S), *ops)


def run_back(core, ge, other, saved, w):
    groups = ge.shape[0]
    steps = groups // NG_B
    ops = list(w)
    packed = jax.ShapeDtypeStruct((PACKED, D), F32)
    out_shape = [jax.ShapeDtypeStruct((groups * NT, S, D), F32), packed, jax.ShapeDtypeStruct((PACKED, D), BF)]
    return pl.pallas_call(
        back_kernel,
        grid_spec=pltpu.PrefetchScalarGridSpec(
            num_scalar_prefetch=1,
            grid=(steps,),
            in_specs=[step_spec((NG_B, D, L)), const_spec(other)] + [step_spec((NG_B,) + v.shape[1:]) for v in saved]
            + [const_spec(o) for o in ops],
            out_specs=[step_spec((NT * NG_B, S, D))] + [const_spec(o) for o in out_shape[1:]],
            scratch_shapes=[pltpu.VMEM((PACKED, D), F32)] + [pltpu.VMEM(shape, dt) for shape, dt in ACC] + prep_scratch()
            + scratch_of(BACK, NG_B),
        ),
        out_shape=out_shape,
        compiler_params=PARAMS,
        cost_estimate=cost(20 * 10**9, 60 * 10**6),
    )(core, ge, other, *saved, *ops)


def unpack_kernel(core_ref, mine, other, g_m2, g_m1, g_wi, g_wo, g_gain, g_shift, g_hid, g_mask):
    core = core_ref[0]

    def write(src, l):
        g_m2[l] = src[0:FF, :].astype(F32)
        for j in range(4):
            g_m1[l, :, j * D:(j + 1) * D] = src[FF + j * D:FF + (j + 1) * D, :].astype(F32)
        for j in range(3):
            g_wi[l, :, j * D:(j + 1) * D] = src[2 * FF + j * D:2 * FF + (j + 1) * D, :].astype(F32)
        g_wo[l] = src[2 * FF + 3 * D:SMALL, :].astype(F32)
        rows = src[SMALL:SMALL + 16, :].astype(F32)
        g_gain[l] = rows[0:2]
        g_shift[l] = rows[2:6]
        for j in range(4):
            g_hid[l:l + 1, j * D:(j + 1) * D] = rows[6 + j:7 + j]
        if l == 1:
            g_mask[...] = rows[10:11]

    @pl.when(core == 0)
    def _():
        write(mine, 0)
        write(other, 1)

    @pl.when(core == 1)
    def _():
        write(other, 0)
        write(mine, 1)


def unpack(core, mine, other):
    shapes = [(2, FF, D), (2, D, FF), (2, D, 3 * D), (2, D, D), (2, 2, D), (2, 4, D), (2, FF), (1, D)]
    return pl.pallas_call(
        unpack_kernel,
        grid_spec=pltpu.PrefetchScalarGridSpec(
            num_scalar_prefetch=1,
            grid=(1,),
            in_specs=[const_spec(mine), const_spec(other)],
            out_specs=[pl.BlockSpec(sh, lambda *_, n=len(sh): (0,) * n) for sh in shapes],
        ),
        out_shape=[jax.ShapeDtypeStruct(sh, F32) for sh in shapes],
        compiler_params=PARAMS,
    )(core.reshape(1).astype(jnp.int32), mine, other)


def partner(i, first, second, n_group):
    dp, x = i // n_group, i % n_group
    y, z, core = dp // 8, dp % 8 // 2, dp % 2
    axis, bits = second if core else first
    if axis == "x":
        x ^= bits
    elif axis == "y":
        y ^= bits
    else:
        z ^= bits
    return (y * 8 + z * 2 + core) * n_group + x


def swap(value, first, second, n_dp, n_group):
    pairs = [(i, partner(i, first, second, n_group)) for i in range(n_dp * n_group)]
    return lax.ppermute(value, ("dp", "group"), pairs)


def swap_cores(value, n_dp):
    return lax.ppermute(value, "dp", [(i, i ^ 1) for i in range(n_dp)])


def split(value, bit):
    half = value.shape[0] // 2
    keep = lax.dynamic_slice_in_dim(value, bit * half, half, axis=0)
    send = lax.dynamic_slice_in_dim(value, (1 - bit) * half, half, axis=0)
    return keep, send.astype(BF)


def join(mine, other, bit):
    return jnp.where(bit == 0, jnp.concatenate([mine, other], axis=0), jnp.concatenate([other, mine], axis=0))


def reduce_all(core, keep, send, n_dp, n_group):
    place = jnp.where(core == 0, lax.axis_index("group"), lax.axis_index("dp") // 8)
    value = keep + swap_cores(send, n_dp).astype(F32)
    for bits, bit in ((3, place // 2), (1, place % 2)):
        keep, send = split(value, bit)
        value = keep + swap(send, ("x", bits), ("y", bits), n_dp, n_group).astype(F32)
    for first, second in (("y", "z"), ("z", "x")):
        for bits in (3, 1):
            value = value + swap(value.astype(BF), (first, bits), (second, bits), n_dp, n_group).astype(F32)
    value = value.astype(BF)
    for bits, bit in ((1, place % 2), (3, place // 2)):
        value = join(value, swap(value, ("x", bits), ("y", bits), n_dp, n_group), bit)
    return value, swap_cores(value, n_dp)


def on_device(token_tiles, segment_ids, visible_flags, tile_order, mask_token, norm_gains, shift_terms,
              attn_in, attn_out, mlp_in, hidden_shift, mlp_out, cotangent):
    tiles = token_tiles.shape[2]
    full_shape = (1, 1, tiles, S, D)
    order = tile_order.reshape(tiles)
    spots = jnp.arange(tiles, dtype=jnp.int32)
    inv_order = jnp.sum(jnp.where(order[None, :] == spots[:, None], spots[None, :], 0), axis=1).astype(jnp.int32)
    cot = lax.all_to_all(cotangent.reshape(tiles, S, D), "dp", split_axis=0, concat_axis=0, tiled=True)
    w = (norm_gains, shift_terms, hidden_shift, attn_in, attn_out, mlp_in, mlp_out)
    seg, vis = segment_ids.reshape(tiles, S), visible_flags.reshape(tiles, S)
    enc, *saved = run_encode(token_tiles.reshape(tiles, S, D), seg, vis, w)
    dec, ge, packed1 = run_decode(inv_order, enc, cot, seg, vis, mask_token.reshape(1, D), w)
    decoded = lax.all_to_all(dec, "dp", split_axis=0, concat_axis=0, tiled=True)
    core = lax.rem(lax.axis_index("dp"), 2).astype(jnp.int32)
    tg, keep, send = run_back(core.reshape(1), ge, packed1, saved, w)
    n_dp = lax.axis_size("dp")
    if n_dp == 32:
        decoded, send = lax.optimization_barrier((decoded, send))
        mine, other = reduce_all(core, keep, send, n_dp, lax.axis_size("group"))
    else:
        mine, other = keep.astype(BF), send
    g_m2, g_m1, g_wi, g_wo, g_gain, g_shift, g_hid, g_mask = unpack(core, mine, other)
    return (
        decoded.reshape(full_shape),
        tg.reshape(full_shape),
        g_mask.reshape(D),
        g_gain,
        g_shift,
        g_wi,
        g_wo,
        g_m1,
        g_hid,
        g_m2,
    )


def solution(mesh):
    tile5 = P("dp", "group", None, None, None)
    in_specs = (tile5, P("dp", "group", None, None), P("dp", "group", None, None), P("dp", "group", None),
                P(), P(), P(), P(), P(), P(), P(), P(), tile5)
    out_specs = (tile5, tile5) + (P(),) * 8
    return jax.shard_map(on_device, mesh=mesh, in_specs=in_specs, out_specs=out_specs, check_vma=False)
```

```python
import jax
import jax.numpy as jnp
from jax import lax
from jax.experimental import pallas as pl
from jax.experimental.pallas import tpu as pltpu
from jax.sharding import PartitionSpec as P

HEADS = 8
HEAD = 16
D = 128
FF = 512
S = 128
NT = 2
NG_E = 8
TURN_E = 2
TURN_D = 2
TURN_B = 2
NG_D = 8
NG_B = 4
L = NT * S
SMALL = 2 * FF + 4 * D
PACKED = SMALL + 64
EPS = 1e-5
LOG2E = 1.4426950408889634
LN2 = 0.6931471805599453
F32 = jnp.float32
BF = jnp.bfloat16


def nn(a, b):
    return lax.dot_general(a, b, (((1,), (0,)), ((), ())), preferred_element_type=F32)


def nt(a, b):
    return lax.dot_general(a, b, (((1,), (1,)), ((), ())), preferred_element_type=F32)


def wide(col):
    return jnp.concatenate([col] * NT, axis=1)


def fold(val):
    out = val[:, :S]
    for t in range(1, NT):
        out = out + val[:, t * S:(t + 1) * S]
    return out


def normalize(x):
    center = x - jnp.sum(x, axis=0, keepdims=True) * (1.0 / D)
    var = jnp.sum(center * center, axis=0, keepdims=True) * (1.0 / D)
    rstd = lax.rsqrt(var + EPS)
    return center * rstd, rstd


def norm_back(grad, xhat, rstd, gain):
    gx = grad * gain
    m1 = jnp.sum(gx, axis=0, keepdims=True) * (1.0 / D)
    m2 = jnp.sum(gx * xhat, axis=0, keepdims=True) * (1.0 / D)
    return (gx - m1 - xhat * m2) * rstd


def padded(rows, h):
    parts = []
    if h > 0:
        parts.append(jnp.zeros((HEAD * h, S), BF))
    parts.append(rows)
    if h < HEADS - 1:
        parts.append(jnp.zeros((D - HEAD * (h + 1), S), BF))
    return jnp.concatenate(parts, axis=0)


def pair_rhs(two, h):
    return jnp.concatenate([padded(two[0:HEAD], h), padded(two[HEAD:2 * HEAD], h + 1)], axis=1)


def flip_pair(two):
    return jnp.concatenate([jnp.transpose(two[:, 0:S]), jnp.transpose(two[:, S:2 * S])], axis=1)


def quad_lhs(one, two):
    zero = jnp.zeros_like(one)
    return jnp.concatenate(
        [jnp.concatenate([one, zero], axis=1), jnp.concatenate([zero, two], axis=1)], axis=0)


def pair_lhs(two):
    zero = jnp.zeros((HEAD, S), BF)
    return jnp.concatenate(
        [jnp.concatenate([two[0:HEAD], zero], axis=1), jnp.concatenate([zero, two[HEAD:2 * HEAD]], axis=1)], axis=0)


UNITS = [(t, h) for t in range(NT) for h in range(0, HEADS, 2)]


def mix_values(sv, t, h):
    sl = slice(t * S, (t + 1) * S)
    v = [sv["p"][2 * D + HEAD * (h + 2 * q):2 * D + HEAD * (h + 2 * q + 2), sl] for q in range(2)]
    ones = jnp.ones((HEAD // 2, S), BF)
    left = jnp.concatenate([quad_lhs(*v), quad_lhs(ones, ones)], axis=0)
    o = nn(left, jnp.concatenate([sv["e"][t, :, (h + 2 * q) * S:(h + 2 * q + 2) * S] for q in range(2)], axis=0))
    totals = []
    for k in range(4):
        kl = slice(k % 2 * S, (k % 2 + 1) * S)
        totals.append(o[4 * HEAD + 8 * (k // 2):4 * HEAD + 8 * (k // 2) + 8, kl])
        inv = 1.0 / totals[k]
        sv["inv"][8 * (h + k):8 * (h + k) + 8, sl] = inv
        sv["o"][HEAD * (h + k):HEAD * (h + k + 1), sl] = (
            o[HEAD * k:HEAD * (k + 1), kl] * jnp.concatenate([inv, inv], axis=0)).astype(BF)
    return totals


def redo_shifted(low, high, group_view, group_bias, ng):
    safe = (jnp.min(low) > 2.0 ** -60) & (jnp.max(high) < 2.0 ** 60)

    @pl.when(jnp.logical_not(safe))
    def _():
        def one(g, carry):
            sv = group_view(g)
            biases = group_bias(g)
            for t, h in UNITS:
                sl = slice(t * S, (t + 1) * S)
                keys = jnp.transpose(sv["p"][D:2 * D, sl])
                scores = nn(keys, pair_rhs(sv["p"][HEAD * h:HEAD * (h + 2), sl], h))
                for k in range(2):
                    part = scores[:, k * S:(k + 1) * S] + biases[t]
                    e = jnp.exp2(part - jnp.max(part, axis=0, keepdims=True))
                    sv["e"][t, :, (h + k) * S:(h + k + 1) * S] = e.astype(BF)
                if h % 4:
                    mix_values(sv, t, h - 2)
            return carry

        lax.fori_loop(0, ng, one, 0)


def layer_fwd(x, biases, w, sv, share):
    per_turn = share["per_turn"]
    wi_t, wo_t, m1_t, m2_t, cols = w["wi_t"], w["wo_t"], w["m1_t"], w["m2_t"], w["cols"]
    xhat0, rstd0 = normalize(x)
    sv["xhat0"][...] = xhat0.astype(BF)
    sv["rstd"][0:8, :] = jnp.broadcast_to(rstd0, (8, L))
    a = (xhat0 * wide(cols[0]) + wide(cols[2])).astype(BF)
    sv["a"][...] = a
    p = nn(wi_t[...], a)
    yield
    sv["p"][0:D, :] = (p[0:D] * (0.25 * LOG2E)).astype(BF)
    sv["p"][D:3 * D, :] = p[D:3 * D].astype(BF)
    yield
    keys = [jnp.transpose(sv["p"][D:2 * D, t * S:(t + 1) * S]) for t in range(NT)]
    n = len(UNITS)
    for turn in range(0, n + per_turn, per_turn):
        for t, h in UNITS[turn:turn + per_turn]:
            scores = nn(keys[t], pair_rhs(sv["p"][HEAD * h:HEAD * (h + 2), t * S:(t + 1) * S], h))
            for k in range(2):
                e = jnp.exp2(scores[:, k * S:(k + 1) * S] + biases[t])
                sv["e"][t, :, (h + k) * S:(h + k + 1) * S] = e.astype(BF)
        for t, h in UNITS[max(turn - per_turn, 0):turn:2]:
            for total in mix_values(sv, t, h):
                share["low"] = total if share["low"] is None else jnp.minimum(share["low"], total)
                share["high"] = total if share["high"] is None else jnp.maximum(share["high"], total)
        yield
    if share["last"] is sv:
        share["redo"](share["low"], share["high"])
    yield
    x1 = x + nn(wo_t[...], sv["o"][...]) + wide(cols[4])
    yield
    xhat1, rstd1 = normalize(x1)
    sv["xhat1"][...] = xhat1.astype(BF)
    sv["rstd"][8:16, :] = jnp.broadcast_to(rstd1, (8, L))
    b = (xhat1 * wide(cols[1]) + wide(cols[3])).astype(BF)
    sv["b"][...] = b
    yield
    b = jnp.concatenate([b, jnp.ones((HEAD, L), BF)], axis=0)
    hidden = None
    for i in range(5):
        last = hidden
        if i < 4:
            hidden = nn(m1_t[i * D:(i + 1) * D, 0:D + HEAD], b)
        if i >= 1:
            rows = slice((i - 1) * D, i * D)
            hv = last
            arg = hv * 0.7071067811865476
            cdf2 = lax.erf(arg) + 1.0
            sv["u"][rows, :] = (hv * cdf2).astype(BF)
            bell = jnp.exp2(arg * arg * -LOG2E)
            sv["gp"][rows, :] = (cdf2 + arg * 1.1283791670955126 * bell).astype(BF)
        yield
    return x1 + nn(m2_t[...], sv["u"][...]) + wide(cols[5])


def lanes(views, name):
    return jnp.concatenate([sv[name][...] for sv in views], axis=1)


def layer_bwd(g2, w, sv, acc, share):
    wi, wo, m1, m2, cols = w["wi"], w["wo"], w["m1"], w["m2_h"], w["cols"]
    a_vec, a_wi, a_wo, a_m1, a_m2 = acc
    views = share["views"]
    per_turn = share["per_turn"]
    last = views[-1] is sv
    n = len(UNITS)
    gz = g2.astype(BF)
    sv["gz"][...] = gz
    gu = None
    for i in range(3):
        done = gu
        if i < 2:
            gu = nn(m2[i * 2 * D:(i + 1) * 2 * D, :], gz)
        if i >= 1:
            rows = slice((i - 1) * 2 * D, i * 2 * D)
            sv["gh"][rows, :] = (done * sv["gp"][rows, :].astype(F32)).astype(BF)
        yield
    gb = nn(m1[...], sv["gh"][...])
    yield
    if last:
        width = L * len(views)
        a_m2[...] += nt(jnp.concatenate([lanes(views, "u"), jnp.ones((HEAD, width), BF)], axis=0), lanes(views, "gz"))
    yield
    if last:
        a_m1[...] += nt(lanes(views, "gh"), jnp.concatenate([lanes(views, "b"), jnp.ones((D, width), BF)], axis=0))
    yield
    xhat1 = sv["xhat1"][...].astype(F32)
    a_vec[1] += fold(gb * xhat1)
    a_vec[3] += fold(gb)
    g1 = g2 + norm_back(gb, xhat1, sv["rstd"][8:9, :], wide(cols[1]))
    gy = g1.astype(BF)
    sv["gy"][...] = gy
    yield
    go = nn(wo[...], gy)
    yield
    if last:
        a_wo[...] += nt(jnp.concatenate([lanes(views, "o"), jnp.ones((HEAD, width), BF)], axis=0), lanes(views, "gy"))
    values = [jnp.transpose(sv["p"][2 * D:3 * D, t * S:(t + 1) * S]) for t in range(NT)]
    gobs = {}
    for turn in range(0, n + per_turn, per_turn):
        for i in range(turn, min(turn + per_turn, n)):
            t, h = UNITS[i]
            sl = slice(t * S, (t + 1) * S)
            parts, rs = [], []
            for k in (h, h + 1):
                hs = slice(HEAD * k, HEAD * (k + 1))
                inv = sv["inv"][8 * k:8 * k + 8, sl]
                gob = (go[hs, sl] * jnp.concatenate([inv, inv], axis=0)).astype(BF)
                parts.append(gob)
                rs.append(jnp.sum(gob.astype(F32) * sv["o"][hs, sl].astype(F32), axis=0, keepdims=True))
            gobs[i] = jnp.concatenate(parts, axis=0)
            gf = nn(values[t], pair_rhs(gobs[i], h))
            for k in range(2):
                kl = slice(k * S, (k + 1) * S)
                e = sv["e"][t, :, (h + k) * S:(h + k + 1) * S].astype(F32)
                sv["gs"][i, :, kl] = (e * (gf[:, kl] - rs[k])).astype(BF)
        for i in range(max(turn - per_turn, 0), turn, 2):
            t, h = UNITS[i]
            sl = slice(t * S, (t + 1) * S)
            gs2 = [sv["gs"][i], sv["gs"][i + 1]]
            e2 = [sv["e"][t, :, (h + 2 * q) * S:(h + 2 * q + 2) * S] for q in range(2)]
            pv = nn(quad_lhs(gobs[i], gobs[i + 1]), jnp.concatenate([flip_pair(v) for v in e2], axis=0))
            pq = nn(quad_lhs(*[sv["p"][D + HEAD * (h + 2 * q):D + HEAD * (h + 2 * q + 2), sl] for q in range(2)]),
                    jnp.concatenate(gs2, axis=0))
            pk = nn(quad_lhs(*[sv["p"][HEAD * (h + 2 * q):HEAD * (h + 2 * q + 2), sl] for q in range(2)]),
                    jnp.concatenate([flip_pair(v) for v in gs2], axis=0))
            for k in range(4):
                kr = slice(HEAD * k, HEAD * (k + 1))
                kl = slice(k % 2 * S, (k % 2 + 1) * S)
                at = HEAD * (h + k)
                sv["gpk"][at:at + HEAD, sl] = (pq[kr, kl] * 0.25).astype(BF)
                sv["gpk"][D + at:D + at + HEAD, sl] = (pk[kr, kl] * LN2).astype(BF)
                sv["gpk"][2 * D + at:2 * D + at + HEAD, sl] = pv[kr, kl].astype(BF)
        yield
    ga = nn(wi[...], sv["gpk"][...])
    yield
    if last:
        a_wi[...] += nt(lanes(views, "gpk"), lanes(views, "a"))
    xhat0 = sv["xhat0"][...].astype(F32)
    a_vec[0] += fold(ga * xhat0)
    a_vec[2] += fold(ga)
    return g1 + norm_back(ga, xhat0, sv["rstd"][0:1, :], wide(cols[0]))


def masks(seg_ref, vis_ref, first, decoder):
    rows_i = lax.broadcasted_iota(jnp.int32, (S, S), 0)
    cols_i = lax.broadcasted_iota(jnp.int32, (S, S), 1)
    diag = rows_i == cols_i
    out = []
    for t in range(NT):
        seg = seg_ref[0, pl.ds(first + t, 1), :]
        key = jnp.where(seg >= 0, seg, -2)
        if not decoder:
            key = jnp.where(vis_ref[0, pl.ds(first + t, 1), :] == 1, key, -2)
        key_k = jnp.transpose(jnp.broadcast_to(key, (S, S)).astype(F32))
        out.append(jnp.where((key_k == seg.astype(F32)) | diag, 0.0, -1e30))
    return out


def drive(gens):
    gens = list(gens)
    while gens:
        alive = []
        for gen in gens:
            try:
                next(gen)
                alive.append(gen)
            except StopIteration:
                pass
        gens = alive


SAVED = {
    "p": ((3 * D, L), BF),
    "e": ((NT, S, HEADS * S), BF),
    "inv": ((8 * HEADS, L), F32),
    "o": ((D, L), BF),
    "u": ((FF, L), BF),
    "gp": ((FF, L), BF),
    "xhat0": ((D, L), BF),
    "xhat1": ((D, L), BF),
    "a": ((D, L), BF),
    "b": ((D, L), BF),
    "rstd": ((16, L), F32),
}
BACK = {
    "gs": ((len(UNITS), S, 2 * S), BF),
    "gz": ((D, L), BF),
    "gy": ((D, L), BF),
    "gh": ((FF, L), BF),
    "gpk": ((3 * D, L), BF),
}
RAW = ("gains", "shifts", "hidden", "wi", "wo", "m1", "m2")
PREP = {
    "cols": ((6, D, S), F32),
    "wi_t": ((3 * D, D), BF),
    "wo_t": ((D, D), BF),
    "m1_t": ((FF, 2 * D), BF),
    "m2_t": ((D, FF), BF),
    "m2_h": ((FF, D), BF),
}


def spread_row(row):
    return jnp.transpose(jnp.broadcast_to(row, (S, D)))


def prep_weights(l, raw, prep, forward):
    raw = dict(zip(RAW, raw))
    prep = dict(zip(PREP, prep))

    @pl.when(pl.program_id(0) == 0)
    def _():
        for j in range(2):
            prep["cols"][j] = spread_row(raw["gains"][l, j:j + 1, :])
        for j in range(4):
            prep["cols"][2 + j] = spread_row(raw["shifts"][l, j:j + 1, :])
        if forward:
            for j in range(4):
                rows = slice(j * D, (j + 1) * D)
                prep["m1_t"][rows, 0:D] = jnp.transpose(raw["m1"][l, :, rows])
                bias = spread_row(raw["hidden"][l:l + 1, rows])
                high = bias.astype(BF)
                mid = (bias - high.astype(F32)).astype(BF)
                low = (bias - high.astype(F32) - mid.astype(F32)).astype(BF)
                lane = lax.broadcasted_iota(jnp.int32, (D, S), 1)
                terms = jnp.where(lane == 0, high.astype(F32), 0.0) + jnp.where(lane == 1, mid.astype(F32), 0.0)
                prep["m1_t"][rows, D:2 * D] = (terms + jnp.where(lane == 2, low.astype(F32), 0.0)).astype(BF)
                prep["m2_t"][:, rows] = jnp.transpose(raw["m2"][l, rows, :]) * BF(0.5)
            for j in range(3):
                rows = slice(j * D, (j + 1) * D)
                prep["wi_t"][rows, :] = jnp.transpose(raw["wi"][l, :, rows])
            prep["wo_t"][...] = jnp.transpose(raw["wo"][l])
        prep["m2_h"][...] = raw["m2"][l] * BF(0.5)

    return prep | {name: raw[name].at[l] for name in ("wi", "wo", "m1")}


def scratch_of(table, ng):
    return [pltpu.VMEM((ng,) + shape, dt) for shape, dt in table.values()]


def prep_scratch():
    return [pltpu.VMEM(shape, dt) for shape, dt in PREP.values()]


def views(names, refs, g):
    return {name: ref.at[g] for name, ref in zip(names, refs)}


def sharing(group_views, per_turn, view_at, bias_at):
    return {
        "per_turn": per_turn,
        "views": group_views,
        "last": group_views[-1],
        "low": None,
        "high": None,
        "redo": lambda low, high: redo_shifted(low, high, view_at, bias_at, len(group_views)),
    }


def encode_kernel(x_ref, seg_ref, vis_ref, *rest):
    raw, rest = rest[:len(RAW)], rest[len(RAW):]
    enc_ref = rest[0]
    saved = rest[1:1 + len(SAVED)]
    w = prep_weights(0, raw, rest[1 + len(SAVED):], True)
    share = sharing([views(SAVED, saved, g) for g in range(NG_E)], TURN_E, lambda g: views(SAVED, saved, g),
                    lambda g: masks(seg_ref, vis_ref, NT * g, False))

    def group(g):
        sv = share["views"][g]
        bias = masks(seg_ref, vis_ref, NT * g, False)
        x = jnp.concatenate([jnp.transpose(x_ref[NT * g + t]).astype(F32) for t in range(NT)], axis=1)
        yield
        out = yield from layer_fwd(x, bias, w, sv, share)
        enc_ref[g] = out.astype(BF)

    drive([group(g) for g in range(NG_E)])


def zero_first(refs):
    @pl.when(pl.program_id(0) == 0)
    def _():
        for ref in refs:
            ref[...] = jnp.zeros_like(ref)


ACC = [
    ((4, D, S), F32),
    ((3 * D, D), F32),
    ((D + HEAD, D), F32),
    ((FF, 2 * D), F32),
    ((FF + HEAD, D), F32),
]


def finish(acc, out, a_mask=None):
    a_vec, a_wi, a_wo, a_m1, a_m2 = acc

    @pl.when(pl.program_id(0) == pl.num_programs(0) - 1)
    def _():
        out[0:FF, :] = a_m2[0:FF, :] * 0.5
        for j in range(4):
            rows = slice(j * D, (j + 1) * D)
            out[FF + j * D:FF + (j + 1) * D, :] = jnp.transpose(a_m1[rows, 0:D])
            out[SMALL + 6 + j:SMALL + 7 + j, :] = jnp.transpose(a_m1[rows, D:2 * D])[0:1]
            out[SMALL + j:SMALL + j + 1, :] = jnp.sum(jnp.transpose(a_vec[j]), axis=0, keepdims=True)
        for j in range(3):
            rows = slice(j * D, (j + 1) * D)
            out[2 * FF + j * D:2 * FF + (j + 1) * D, :] = jnp.transpose(a_wi[rows, :])
        out[2 * FF + 3 * D:SMALL, :] = a_wo[0:D, :]
        out[SMALL + 4:SMALL + 5, :] = a_wo[D:D + 1, :]
        out[SMALL + 5:SMALL + 6, :] = a_m2[FF:FF + 1, :]
        out[SMALL + 11:PACKED, :] = jnp.zeros((PACKED - SMALL - 11, D), F32)
        out[SMALL + 10:SMALL + 11, :] = jnp.zeros((1, D), F32)
        if a_mask is not None:
            out[SMALL + 10:SMALL + 11, :] = jnp.sum(jnp.transpose(a_mask[...]), axis=0, keepdims=True)


def decode_kernel(inv_order, enc_ref, *rest):
    cots = rest[:(NT * NG_D)]
    seg_ref, vis_ref, mask_row = rest[(NT * NG_D):(NT * NG_D) + 3]
    rest = rest[(NT * NG_D) + 3:]
    raw, rest = rest[:len(RAW)], rest[len(RAW):]
    dec_out, ge_ref, out_ref = rest[:3]
    rest = rest[3:]
    acc, rest = rest[:len(ACC)], rest[len(ACC):]
    a_mask, maskcol, dec_ref, sems = rest[:4]
    rest = rest[4:]
    w = prep_weights(1, raw, rest[:len(PREP)], True)
    scr = rest[len(PREP):]
    step = pl.program_id(0)
    slot = lax.rem(step, 2)

    @pl.when(step == 0)
    def _():
        maskcol[...] = spread_row(mask_row[0:1, :])

    def copies(at, where):
        return [
            pltpu.make_async_copy(dec_ref.at[where, t], dec_out.at[inv_order[(NT * NG_D) * at + t]], sems.at[where, t])
            for t in range((NT * NG_D))
        ]

    @pl.when(step >= 2)
    def _():
        for copy in copies(step - 2, slot):
            copy.wait()

    zero_first(acc + (a_mask,))
    table = list(SAVED) + list(BACK)
    share = sharing([views(table, scr, g) for g in range(NG_D)], TURN_D, lambda g: views(table, scr, g),
                    lambda g: masks(seg_ref, vis_ref, NT * g, True))

    def group(g):
        sv = share["views"][g]
        bias = masks(seg_ref, vis_ref, NT * g, True)
        shown = jnp.concatenate([vis_ref[0, NT * g + t:NT * g + t + 1, :] for t in range(NT)], axis=1) == 1
        x = jnp.where(shown, enc_ref[g].astype(F32), wide(maskcol[...]))
        yield
        out = yield from layer_fwd(x, bias, w, sv, share)
        outb = out.astype(BF)
        for t in range(NT):
            dec_ref[slot, NT * g + t] = jnp.transpose(outb[:, t * S:(t + 1) * S])
        yield
        grad = jnp.concatenate([jnp.transpose(cots[NT * g + t][0]).astype(F32) for t in range(NT)], axis=1)
        yield
        grad = yield from layer_bwd(grad, w, sv, acc, share)
        a_mask[...] += fold(jnp.where(shown, 0.0, grad))
        ge_ref[g] = jnp.where(shown, grad, 0.0).astype(BF)

    drive([group(g) for g in range(NG_D)])
    for copy in copies(step, slot):
        copy.start()

    @pl.when(step == pl.num_programs(0) - 1)
    def _():
        for copy in copies(step - 1, 1 - slot) + copies(step, slot):
            copy.wait()

    finish(acc, out_ref, a_mask)


def back_kernel(core_ref, ge_ref, other_ref, *rest):
    saved = rest[:len(SAVED)]
    rest = rest[len(SAVED):]
    raw, rest = rest[:len(RAW)], rest[len(RAW):]
    tg_ref, keep_ref, send_ref = rest[:3]
    out_ref, rest = rest[3], rest[4:]
    acc, rest = rest[:len(ACC)], rest[len(ACC):]
    w = prep_weights(0, raw, rest[:len(PREP)], False)
    scr = rest[len(PREP):]
    zero_first(acc)
    share = sharing([views(SAVED, saved, g) | views(BACK, scr, g) for g in range(NG_B)], TURN_B, None, None)

    def group(g):
        sv = share["views"][g]
        grad = ge_ref[g].astype(F32)
        yield
        grad = yield from layer_bwd(grad, w, sv, acc, share)
        for t in range(NT):
            tg_ref[NT * g + t] = jnp.transpose(grad[:, t * S:(t + 1) * S])

    drive([group(g) for g in range(NG_B)])
    finish(acc, out_ref)

    @pl.when((pl.program_id(0) == pl.num_programs(0) - 1) & (core_ref[0] == 0))
    def _():
        keep_ref[...] = out_ref[...]
        send_ref[...] = other_ref[...].astype(BF)

    @pl.when((pl.program_id(0) == pl.num_programs(0) - 1) & (core_ref[0] == 1))
    def _():
        keep_ref[...] = other_ref[...]
        send_ref[...] = out_ref[...].astype(BF)


def const_spec(arr):
    return pl.BlockSpec(arr.shape, lambda *_: (0,) * arr.ndim)


def step_spec(shape):
    return pl.BlockSpec(shape, lambda i, *_: (i,) + (0,) * (len(shape) - 1))


PARAMS = pltpu.CompilerParams(dimension_semantics=("arbitrary",), vmem_limit_bytes=60 * 1024 * 1024)
GRADS = [jax.ShapeDtypeStruct((PACKED, D), F32)]


def cost(flops, nbytes):
    return pl.CostEstimate(flops=flops, bytes_accessed=nbytes, transcendentals=0)


def run_encode(x, seg, vis, w):
    tiles = x.shape[0]
    groups, steps = tiles // NT, tiles // (NT * NG_E)
    ops = list(w)
    out_shape = [jax.ShapeDtypeStruct((groups, D, L), BF)]
    out_shape += [jax.ShapeDtypeStruct((groups,) + shape, dt) for shape, dt in SAVED.values()]
    return pl.pallas_call(
        encode_kernel,
        grid=(steps,),
        in_specs=[step_spec(((NT * NG_E), S, D)), step_spec((1, (NT * NG_E), S)), step_spec((1, (NT * NG_E), S))] + [const_spec(o) for o in ops],
        out_specs=[step_spec((NG_E,) + o.shape[1:]) for o in out_shape],
        out_shape=out_shape,
        scratch_shapes=prep_scratch(),
        cost_estimate=cost(20 * 10**9, 60 * 10**6),
        compiler_params=PARAMS,
    )(x, seg.reshape(steps, (NT * NG_E), S), vis.reshape(steps, (NT * NG_E), S), *ops)


def run_decode(inv_order, enc, cot, seg, vis, mask_row, w):
    tiles = cot.shape[0]
    groups, steps = tiles // NT, tiles // (NT * NG_D)
    ops = [mask_row] + list(w)
    cot_specs = [pl.BlockSpec((1, S, D), lambda i, o, t=t: (o[(NT * NG_D) * i + t], 0, 0)) for t in range((NT * NG_D))]
    out_shape = [jax.ShapeDtypeStruct((tiles, S, D), BF), jax.ShapeDtypeStruct((groups, D, L), BF)] + GRADS
    return pl.pallas_call(
        decode_kernel,
        grid_spec=pltpu.PrefetchScalarGridSpec(
            num_scalar_prefetch=1,
            grid=(steps,),
            in_specs=[step_spec((NG_D, D, L))] + cot_specs + [step_spec((1, (NT * NG_D), S))] * 2 + [const_spec(o) for o in ops],
            out_specs=[pl.BlockSpec(memory_space=pl.ANY), step_spec((NG_D, D, L))] + [const_spec(o) for o in GRADS],
            scratch_shapes=[pltpu.VMEM(shape, dt) for shape, dt in ACC] + [pltpu.VMEM((D, S), F32)] * 2
            + [pltpu.VMEM((2, (NT * NG_D), S, D), BF), pltpu.SemaphoreType.DMA((2, (NT * NG_D)))]
            + prep_scratch() + scratch_of(SAVED, NG_D) + scratch_of(BACK, NG_D),
        ),
        out_shape=out_shape,
        cost_estimate=cost(40 * 10**9, 10 * 10**6),
        compiler_params=PARAMS,
    )(inv_order, enc, *([cot] * (NT * NG_D)), seg.reshape(steps, (NT * NG_D), S), vis.reshape(steps, (NT * NG_D), S), *ops)


def run_back(core, ge, other, saved, w):
    groups = ge.shape[0]
    steps = groups // NG_B
    ops = list(w)
    packed = jax.ShapeDtypeStruct((PACKED, D), F32)
    out_shape = [jax.ShapeDtypeStruct((groups * NT, S, D), F32), packed, jax.ShapeDtypeStruct((PACKED, D), BF)]
    return pl.pallas_call(
        back_kernel,
        grid_spec=pltpu.PrefetchScalarGridSpec(
            num_scalar_prefetch=1,
            grid=(steps,),
            in_specs=[step_spec((NG_B, D, L)), const_spec(other)] + [step_spec((NG_B,) + v.shape[1:]) for v in saved]
            + [const_spec(o) for o in ops],
            out_specs=[step_spec((NT * NG_B, S, D))] + [const_spec(o) for o in out_shape[1:]],
            scratch_shapes=[pltpu.VMEM((PACKED, D), F32)] + [pltpu.VMEM(shape, dt) for shape, dt in ACC] + prep_scratch()
            + scratch_of(BACK, NG_B),
        ),
        out_shape=out_shape,
        compiler_params=PARAMS,
        cost_estimate=cost(20 * 10**9, 60 * 10**6),
    )(core, ge, other, *saved, *ops)


def unpack_kernel(core_ref, mine, other, g_m2, g_m1, g_wi, g_wo, g_gain, g_shift, g_hid, g_mask):
    core = core_ref[0]

    def write(src, l):
        g_m2[l] = src[0:FF, :].astype(F32)
        for j in range(4):
            g_m1[l, :, j * D:(j + 1) * D] = src[FF + j * D:FF + (j + 1) * D, :].astype(F32)
        for j in range(3):
            g_wi[l, :, j * D:(j + 1) * D] = src[2 * FF + j * D:2 * FF + (j + 1) * D, :].astype(F32)
        g_wo[l] = src[2 * FF + 3 * D:SMALL, :].astype(F32)
        rows = src[SMALL:SMALL + 16, :].astype(F32)
        g_gain[l] = rows[0:2]
        g_shift[l] = rows[2:6]
        for j in range(4):
            g_hid[l:l + 1, j * D:(j + 1) * D] = rows[6 + j:7 + j]
        if l == 1:
            g_mask[...] = rows[10:11]

    @pl.when(core == 0)
    def _():
        write(mine, 0)
        write(other, 1)

    @pl.when(core == 1)
    def _():
        write(other, 0)
        write(mine, 1)


def unpack(core, mine, other):
    shapes = [(2, FF, D), (2, D, FF), (2, D, 3 * D), (2, D, D), (2, 2, D), (2, 4, D), (2, FF), (1, D)]
    return pl.pallas_call(
        unpack_kernel,
        grid_spec=pltpu.PrefetchScalarGridSpec(
            num_scalar_prefetch=1,
            grid=(1,),
            in_specs=[const_spec(mine), const_spec(other)],
            out_specs=[pl.BlockSpec(sh, lambda *_, n=len(sh): (0,) * n) for sh in shapes],
        ),
        out_shape=[jax.ShapeDtypeStruct(sh, F32) for sh in shapes],
        compiler_params=PARAMS,
    )(core.reshape(1).astype(jnp.int32), mine, other)


def partner(i, first, second, n_group):
    dp, x = i // n_group, i % n_group
    y, z, core = dp // 8, dp % 8 // 2, dp % 2
    axis, bits = second if core else first
    if axis == "x":
        x ^= bits
    elif axis == "y":
        y ^= bits
    else:
        z ^= bits
    return (y * 8 + z * 2 + core) * n_group + x


def swap(value, first, second, n_dp, n_group):
    pairs = [(i, partner(i, first, second, n_group)) for i in range(n_dp * n_group)]
    return lax.ppermute(value, ("dp", "group"), pairs)


def swap_cores(value, n_dp):
    return lax.ppermute(value, "dp", [(i, i ^ 1) for i in range(n_dp)])


def reduce_all(core, keep, send, n_dp, n_group):
    place = jnp.where(core == 0, lax.axis_index("group"), lax.axis_index("dp") // 8)
    value = keep + swap_cores(send, n_dp).astype(F32)
    quarter = value.shape[0] // 4
    whole = value
    value = lax.dynamic_slice_in_dim(whole, place * quarter, quarter, axis=0)
    for bits in (1, 2, 3):
        send = lax.dynamic_slice_in_dim(whole, (place ^ bits) * quarter, quarter, axis=0).astype(BF)
        value = value + swap(send, ("x", bits), ("y", bits), n_dp, n_group).astype(F32)
    for first, second in (("y", "z"), ("z", "x")):
        value = lax.reduce_precision(value, 8, 7)
        one, two, three = [swap(value.astype(BF), (first, bits), (second, bits), n_dp, n_group) for bits in (1, 2, 3)]
        value = (value + one.astype(F32)) + (two.astype(F32) + three.astype(F32))
    value = value.astype(BF)
    pieces = [value] + [swap(value, ("x", bits), ("y", bits), n_dp, n_group) for bits in (1, 2, 3)]
    ordered = []
    for j in range(4):
        away = place ^ j
        low = jnp.where(away == 0, pieces[0], pieces[1])
        ordered.append(jnp.where(away < 2, low, jnp.where(away == 2, pieces[2], pieces[3])))
    value = jnp.concatenate(ordered, axis=0)
    return value, swap_cores(value, n_dp)


def on_device(token_tiles, segment_ids, visible_flags, tile_order, mask_token, norm_gains, shift_terms,
              attn_in, attn_out, mlp_in, hidden_shift, mlp_out, cotangent):
    tiles = token_tiles.shape[2]
    full_shape = (1, 1, tiles, S, D)
    order = tile_order.reshape(tiles)
    spots = jnp.arange(tiles, dtype=jnp.int32)
    inv_order = jnp.sum(jnp.where(order[None, :] == spots[:, None], spots[None, :], 0), axis=1).astype(jnp.int32)
    cot = lax.all_to_all(cotangent.reshape(tiles, S, D), "dp", split_axis=0, concat_axis=0, tiled=True)
    w = (norm_gains, shift_terms, hidden_shift, attn_in, attn_out, mlp_in, mlp_out)
    seg, vis = segment_ids.reshape(tiles, S), visible_flags.reshape(tiles, S)
    enc, *saved = run_encode(token_tiles.reshape(tiles, S, D), seg, vis, w)
    dec, ge, packed1 = run_decode(inv_order, enc, cot, seg, vis, mask_token.reshape(1, D), w)
    decoded = lax.all_to_all(dec, "dp", split_axis=0, concat_axis=0, tiled=True)
    core = lax.rem(lax.axis_index("dp"), 2).astype(jnp.int32)
    tg, keep, send = run_back(core.reshape(1), ge, packed1, saved, w)
    n_dp = lax.axis_size("dp")
    if n_dp == 32:
        decoded, send = lax.optimization_barrier((decoded, send))
        mine, other = reduce_all(core, keep, send, n_dp, lax.axis_size("group"))
    else:
        mine, other = keep.astype(BF), send
    g_m2, g_m1, g_wi, g_wo, g_gain, g_shift, g_hid, g_mask = unpack(core, mine, other)
    return (
        decoded.reshape(full_shape),
        tg.reshape(full_shape),
        g_mask.reshape(D),
        g_gain,
        g_shift,
        g_wi,
        g_wo,
        g_m1,
        g_hid,
        g_m2,
    )


def solution(mesh):
    tile5 = P("dp", "group", None, None, None)
    in_specs = (tile5, P("dp", "group", None, None), P("dp", "group", None, None), P("dp", "group", None),
                P(), P(), P(), P(), P(), P(), P(), P(), tile5)
    out_specs = (tile5, tile5) + (P(),) * 8
    return jax.shard_map(on_device, mesh=mesh, in_specs=in_specs, out_specs=out_specs, check_vma=False)
```

```python
import jax
import jax.numpy as jnp
from jax import lax
from jax.experimental import pallas as pl
from jax.experimental.pallas import tpu as pltpu
from jax.sharding import PartitionSpec as P

HEADS = 8
HEAD = 16
D = 128
FF = 512
S = 128
NT = 2
NG_E = 8
TURN_E = 2
TURN_D = 2
TURN_B = 2
NG_D = 8
NG_B = 4
L = NT * S
SMALL = 2 * FF + 4 * D
PACKED = SMALL + 64
EPS = 1e-5
LOG2E = 1.4426950408889634
LN2 = 0.6931471805599453
F32 = jnp.float32
BF = jnp.bfloat16


def nn(a, b):
    return lax.dot_general(a, b, (((1,), (0,)), ((), ())), preferred_element_type=F32)


def nt(a, b):
    return lax.dot_general(a, b, (((1,), (1,)), ((), ())), preferred_element_type=F32)


def wide(col):
    return jnp.concatenate([col] * NT, axis=1)


def fold(val):
    out = val[:, :S]
    for t in range(1, NT):
        out = out + val[:, t * S:(t + 1) * S]
    return out


def normalize(x):
    center = x - jnp.sum(x, axis=0, keepdims=True) * (1.0 / D)
    var = jnp.sum(center * center, axis=0, keepdims=True) * (1.0 / D)
    rstd = lax.rsqrt(var + EPS)
    return center * rstd, rstd


def norm_back(grad, xhat, rstd, gain):
    gx = grad * gain
    m1 = jnp.sum(gx, axis=0, keepdims=True) * (1.0 / D)
    m2 = jnp.sum(gx * xhat, axis=0, keepdims=True) * (1.0 / D)
    return (gx - m1 - xhat * m2) * rstd


def padded(rows, h):
    parts = []
    if h > 0:
        parts.append(jnp.zeros((HEAD * h, S), BF))
    parts.append(rows)
    if h < HEADS - 1:
        parts.append(jnp.zeros((D - HEAD * (h + 1), S), BF))
    return jnp.concatenate(parts, axis=0)


def pair_rhs(two, h):
    return jnp.concatenate([padded(two[0:HEAD], h), padded(two[HEAD:2 * HEAD], h + 1)], axis=1)


def flip_pair(two):
    return jnp.concatenate([jnp.transpose(two[:, 0:S]), jnp.transpose(two[:, S:2 * S])], axis=1)


def quad_lhs(one, two):
    zero = jnp.zeros_like(one)
    return jnp.concatenate(
        [jnp.concatenate([one, zero], axis=1), jnp.concatenate([zero, two], axis=1)], axis=0)


def pair_lhs(two):
    zero = jnp.zeros((HEAD, S), BF)
    return jnp.concatenate(
        [jnp.concatenate([two[0:HEAD], zero], axis=1), jnp.concatenate([zero, two[HEAD:2 * HEAD]], axis=1)], axis=0)


UNITS = [(t, h) for t in range(NT) for h in range(0, HEADS, 2)]


def mix_values(sv, t, h):
    sl = slice(t * S, (t + 1) * S)
    v = [sv["p"][2 * D + HEAD * (h + 2 * q):2 * D + HEAD * (h + 2 * q + 2), sl] for q in range(2)]
    ones = jnp.ones((HEAD // 2, S), BF)
    left = jnp.concatenate([quad_lhs(*v), quad_lhs(ones, ones)], axis=0)
    o = nn(left, jnp.concatenate([sv["e"][t, :, (h + 2 * q) * S:(h + 2 * q + 2) * S] for q in range(2)], axis=0))
    totals = []
    for k in range(4):
        kl = slice(k % 2 * S, (k % 2 + 1) * S)
        totals.append(o[4 * HEAD + 8 * (k // 2):4 * HEAD + 8 * (k // 2) + 8, kl])
        inv = 1.0 / totals[k]
        sv["inv"][8 * (h + k):8 * (h + k) + 8, sl] = inv
        sv["o"][HEAD * (h + k):HEAD * (h + k + 1), sl] = (
            o[HEAD * k:HEAD * (k + 1), kl] * jnp.concatenate([inv, inv], axis=0)).astype(BF)
    return totals


def redo_shifted(low, high, group_view, group_bias, ng):
    safe = (jnp.min(low) > 2.0 ** -60) & (jnp.max(high) < 2.0 ** 60)

    @pl.when(jnp.logical_not(safe))
    def _():
        def one(g, carry):
            sv = group_view(g)
            biases = group_bias(g)
            for t, h in UNITS:
                sl = slice(t * S, (t + 1) * S)
                keys = jnp.transpose(sv["p"][D:2 * D, sl])
                scores = nn(keys, pair_rhs(sv["p"][HEAD * h:HEAD * (h + 2), sl], h))
                for k in range(2):
                    part = scores[:, k * S:(k + 1) * S] + biases[t]
                    e = jnp.exp2(part - jnp.max(part, axis=0, keepdims=True))
                    sv["e"][t, :, (h + k) * S:(h + k + 1) * S] = e.astype(BF)
                if h % 4:
                    mix_values(sv, t, h - 2)
            return carry

        lax.fori_loop(0, ng, one, 0)


def layer_fwd(x, biases, w, sv, share):
    per_turn = share["per_turn"]
    wi_t, wo_t, m1_t, m2_t, cols = w["wi_t"], w["wo_t"], w["m1_t"], w["m2_t"], w["cols"]
    xhat0, rstd0 = normalize(x)
    sv["xhat0"][...] = xhat0.astype(BF)
    sv["rstd"][0:8, :] = jnp.broadcast_to(rstd0, (8, L))
    a = (xhat0 * wide(cols[0]) + wide(cols[2])).astype(BF)
    sv["a"][...] = a
    p = nn(wi_t[...], a)
    yield
    sv["p"][0:D, :] = (p[0:D] * (0.25 * LOG2E)).astype(BF)
    sv["p"][D:3 * D, :] = p[D:3 * D].astype(BF)
    yield
    keys = [jnp.transpose(sv["p"][D:2 * D, t * S:(t + 1) * S]) for t in range(NT)]
    n = len(UNITS)
    for turn in range(0, n + per_turn, per_turn):
        for t, h in UNITS[turn:turn + per_turn]:
            scores = nn(keys[t], pair_rhs(sv["p"][HEAD * h:HEAD * (h + 2), t * S:(t + 1) * S], h))
            for k in range(2):
                e = jnp.exp2(scores[:, k * S:(k + 1) * S] + biases[t])
                sv["e"][t, :, (h + k) * S:(h + k + 1) * S] = e.astype(BF)
        for t, h in UNITS[max(turn - per_turn, 0):turn:2]:
            for total in mix_values(sv, t, h):
                share["low"] = total if share["low"] is None else jnp.minimum(share["low"], total)
                share["high"] = total if share["high"] is None else jnp.maximum(share["high"], total)
        yield
    if share["last"] is sv:
        share["redo"](share["low"], share["high"])
        share["attended"]()
    yield
    x1 = x + nn(wo_t[...], sv["o"][...]) + wide(cols[4])
    yield
    xhat1, rstd1 = normalize(x1)
    sv["xhat1"][...] = xhat1.astype(BF)
    sv["rstd"][8:16, :] = jnp.broadcast_to(rstd1, (8, L))
    b = (xhat1 * wide(cols[1]) + wide(cols[3])).astype(BF)
    sv["b"][...] = b
    yield
    b = jnp.concatenate([b, jnp.ones((HEAD, L), BF)], axis=0)
    hidden = None
    for i in range(5):
        last = hidden
        if i < 4:
            hidden = nn(m1_t[i * D:(i + 1) * D, 0:D + HEAD], b)
        if i >= 1:
            rows = slice((i - 1) * D, i * D)
            hv = last
            arg = hv * 0.7071067811865476
            cdf2 = lax.erf(arg) + 1.0
            sv["u"][rows, :] = (hv * cdf2).astype(BF)
            bell = jnp.exp2(arg * arg * -LOG2E)
            sv["gp"][rows, :] = (cdf2 + arg * 1.1283791670955126 * bell).astype(BF)
        yield
    return x1 + nn(m2_t[...], sv["u"][...]) + wide(cols[5])


def lanes(views, name):
    return jnp.concatenate([sv[name][...] for sv in views], axis=1)


def layer_bwd(g2, w, sv, acc, share):
    wi, wo, m1, m2, cols = w["wi"], w["wo"], w["m1"], w["m2_h"], w["cols"]
    a_vec, a_wi, a_wo, a_m1, a_m2 = acc
    views = share["views"]
    per_turn = share["per_turn"]
    last = views[-1] is sv
    n = len(UNITS)
    gz = g2.astype(BF)
    sv["gz"][...] = gz
    gu = None
    for i in range(3):
        done = gu
        if i < 2:
            gu = nn(m2[i * 2 * D:(i + 1) * 2 * D, :], gz)
        if i >= 1:
            rows = slice((i - 1) * 2 * D, i * 2 * D)
            sv["gh"][rows, :] = (done * sv["gp"][rows, :].astype(F32)).astype(BF)
        yield
    gb = nn(m1[...], sv["gh"][...])
    yield
    if last:
        width = L * len(views)
        a_m2[...] += nt(jnp.concatenate([lanes(views, "u"), jnp.ones((HEAD, width), BF)], axis=0), lanes(views, "gz"))
    yield
    if last:
        a_m1[...] += nt(lanes(views, "gh"), jnp.concatenate([lanes(views, "b"), jnp.ones((D, width), BF)], axis=0))
    yield
    xhat1 = sv["xhat1"][...].astype(F32)
    a_vec[1] += fold(gb * xhat1)
    a_vec[3] += fold(gb)
    g1 = g2 + norm_back(gb, xhat1, sv["rstd"][8:9, :], wide(cols[1]))
    gy = g1.astype(BF)
    sv["gy"][...] = gy
    yield
    go = nn(wo[...], gy)
    yield
    if last:
        a_wo[...] += nt(jnp.concatenate([lanes(views, "o"), jnp.ones((HEAD, width), BF)], axis=0), lanes(views, "gy"))
    values = [jnp.transpose(sv["p"][2 * D:3 * D, t * S:(t + 1) * S]) for t in range(NT)]
    gobs = {}
    for turn in range(0, n + per_turn, per_turn):
        for i in range(turn, min(turn + per_turn, n)):
            t, h = UNITS[i]
            sl = slice(t * S, (t + 1) * S)
            parts, rs = [], []
            for k in (h, h + 1):
                hs = slice(HEAD * k, HEAD * (k + 1))
                inv = sv["inv"][8 * k:8 * k + 8, sl]
                gob = (go[hs, sl] * jnp.concatenate([inv, inv], axis=0)).astype(BF)
                parts.append(gob)
                rs.append(jnp.sum(gob.astype(F32) * sv["o"][hs, sl].astype(F32), axis=0, keepdims=True))
            gobs[i] = jnp.concatenate(parts, axis=0)
            gf = nn(values[t], pair_rhs(gobs[i], h))
            for k in range(2):
                kl = slice(k * S, (k + 1) * S)
                e = sv["e"][t, :, (h + k) * S:(h + k + 1) * S].astype(F32)
                sv["gs"][i, :, kl] = (e * (gf[:, kl] - rs[k])).astype(BF)
        for i in range(max(turn - per_turn, 0), turn, 2):
            t, h = UNITS[i]
            sl = slice(t * S, (t + 1) * S)
            gs2 = [sv["gs"][i], sv["gs"][i + 1]]
            e2 = [sv["e"][t, :, (h + 2 * q) * S:(h + 2 * q + 2) * S] for q in range(2)]
            pv = nn(quad_lhs(gobs[i], gobs[i + 1]), jnp.concatenate([flip_pair(v) for v in e2], axis=0))
            pq = nn(quad_lhs(*[sv["p"][D + HEAD * (h + 2 * q):D + HEAD * (h + 2 * q + 2), sl] for q in range(2)]),
                    jnp.concatenate(gs2, axis=0))
            pk = nn(quad_lhs(*[sv["p"][HEAD * (h + 2 * q):HEAD * (h + 2 * q + 2), sl] for q in range(2)]),
                    jnp.concatenate([flip_pair(v) for v in gs2], axis=0))
            for k in range(4):
                kr = slice(HEAD * k, HEAD * (k + 1))
                kl = slice(k % 2 * S, (k % 2 + 1) * S)
                at = HEAD * (h + k)
                sv["gpk"][at:at + HEAD, sl] = (pq[kr, kl] * 0.25).astype(BF)
                sv["gpk"][D + at:D + at + HEAD, sl] = (pk[kr, kl] * LN2).astype(BF)
                sv["gpk"][2 * D + at:2 * D + at + HEAD, sl] = pv[kr, kl].astype(BF)
        yield
    ga = nn(wi[...], sv["gpk"][...])
    yield
    if last:
        a_wi[...] += nt(lanes(views, "gpk"), lanes(views, "a"))
    xhat0 = sv["xhat0"][...].astype(F32)
    a_vec[0] += fold(ga * xhat0)
    a_vec[2] += fold(ga)
    return g1 + norm_back(ga, xhat0, sv["rstd"][0:1, :], wide(cols[0]))


def masks(seg_ref, vis_ref, first, decoder):
    rows_i = lax.broadcasted_iota(jnp.int32, (S, S), 0)
    cols_i = lax.broadcasted_iota(jnp.int32, (S, S), 1)
    diag = rows_i == cols_i
    out = []
    for t in range(NT):
        seg = seg_ref[0, pl.ds(first + t, 1), :]
        key = jnp.where(seg >= 0, seg, -2)
        if not decoder:
            key = jnp.where(vis_ref[0, pl.ds(first + t, 1), :] == 1, key, -2)
        key_k = jnp.transpose(jnp.broadcast_to(key, (S, S)).astype(F32))
        out.append(jnp.where((key_k == seg.astype(F32)) | diag, 0.0, -1e30))
    return out


def drive(gens):
    gens = list(gens)
    while gens:
        alive = []
        for gen in gens:
            try:
                next(gen)
                alive.append(gen)
            except StopIteration:
                pass
        gens = alive


SAVED = {
    "p": ((3 * D, L), BF),
    "e": ((NT, S, HEADS * S), BF),
    "inv": ((8 * HEADS, L), F32),
    "o": ((D, L), BF),
    "u": ((FF, L), BF),
    "gp": ((FF, L), BF),
    "xhat0": ((D, L), BF),
    "xhat1": ((D, L), BF),
    "a": ((D, L), BF),
    "b": ((D, L), BF),
    "rstd": ((16, L), F32),
}
LATE = ("xhat1", "b", "u", "gp", "rstd")
BACK = {
    "gs": ((len(UNITS), S, 2 * S), BF),
    "gz": ((D, L), BF),
    "gy": ((D, L), BF),
    "gh": ((FF, L), BF),
    "gpk": ((3 * D, L), BF),
}
RAW = ("gains", "shifts", "hidden", "wi", "wo", "m1", "m2")
PREP = {
    "cols": ((6, D, S), F32),
    "wi_t": ((3 * D, D), BF),
    "wo_t": ((D, D), BF),
    "m1_t": ((FF, 2 * D), BF),
    "m2_t": ((D, FF), BF),
    "m2_h": ((FF, D), BF),
}


def spread_row(row):
    return jnp.transpose(jnp.broadcast_to(row, (S, D)))


def prep_weights(l, raw, prep, forward):
    raw = dict(zip(RAW, raw))
    prep = dict(zip(PREP, prep))

    @pl.when(pl.program_id(0) == 0)
    def _():
        for j in range(2):
            prep["cols"][j] = spread_row(raw["gains"][l, j:j + 1, :])
        for j in range(4):
            prep["cols"][2 + j] = spread_row(raw["shifts"][l, j:j + 1, :])
        if forward:
            for j in range(4):
                rows = slice(j * D, (j + 1) * D)
                prep["m1_t"][rows, 0:D] = jnp.transpose(raw["m1"][l, :, rows])
                bias = spread_row(raw["hidden"][l:l + 1, rows])
                high = bias.astype(BF)
                mid = (bias - high.astype(F32)).astype(BF)
                low = (bias - high.astype(F32) - mid.astype(F32)).astype(BF)
                lane = lax.broadcasted_iota(jnp.int32, (D, S), 1)
                terms = jnp.where(lane == 0, high.astype(F32), 0.0) + jnp.where(lane == 1, mid.astype(F32), 0.0)
                prep["m1_t"][rows, D:2 * D] = (terms + jnp.where(lane == 2, low.astype(F32), 0.0)).astype(BF)
                prep["m2_t"][:, rows] = jnp.transpose(raw["m2"][l, rows, :]) * BF(0.5)
            for j in range(3):
                rows = slice(j * D, (j + 1) * D)
                prep["wi_t"][rows, :] = jnp.transpose(raw["wi"][l, :, rows])
            prep["wo_t"][...] = jnp.transpose(raw["wo"][l])
        prep["m2_h"][...] = raw["m2"][l] * BF(0.5)

    return prep | {name: raw[name].at[l] for name in ("wi", "wo", "m1")}


def scratch_of(table, ng):
    return [pltpu.VMEM((ng,) + shape, dt) for shape, dt in table.values()]


def prep_scratch():
    return [pltpu.VMEM(shape, dt) for shape, dt in PREP.values()]


def views(names, refs, g):
    return {name: ref.at[g] for name, ref in zip(names, refs)}


def sharing(group_views, per_turn, view_at, bias_at):
    return {
        "per_turn": per_turn,
        "views": group_views,
        "last": group_views[-1],
        "low": None,
        "attended": lambda: None,
        "high": None,
        "redo": lambda low, high: redo_shifted(low, high, view_at, bias_at, len(group_views)),
    }


def encode_kernel(x_ref, seg_ref, vis_ref, *rest):
    raw, rest = rest[:len(RAW)], rest[len(RAW):]
    enc_ref = rest[0]
    saved, rest = rest[1:1 + len(SAVED)], rest[1 + len(SAVED):]
    held, rest = rest[:len(SAVED)], rest[len(SAVED):]
    sems, rest = rest[0], rest[1:]
    w = prep_weights(0, raw, rest, True)
    step = pl.program_id(0)
    slot = lax.rem(step, 2)

    def copies(at, where, late):
        return [
            pltpu.make_async_copy(held[j].at[where], saved[j].at[pl.ds(at * NG_E, NG_E)], sems.at[where, j])
            for j, name in enumerate(SAVED) if (name in LATE) == late
        ]

    def start(late):
        for copy in copies(step, slot, late):
            copy.start()

    @pl.when(step >= 2)
    def _():
        for copy in copies(step - 2, slot, False) + copies(step - 2, slot, True):
            copy.wait()

    def view(g):
        return {name: ref.at[slot, g] for name, ref in zip(SAVED, held)}

    share = sharing([view(g) for g in range(NG_E)], TURN_E, view, lambda g: masks(seg_ref, vis_ref, NT * g, False))
    share["attended"] = lambda: start(False)

    def group(g):
        sv = share["views"][g]
        bias = masks(seg_ref, vis_ref, NT * g, False)
        x = jnp.concatenate([jnp.transpose(x_ref[NT * g + t]).astype(F32) for t in range(NT)], axis=1)
        yield
        out = yield from layer_fwd(x, bias, w, sv, share)
        enc_ref[g] = out.astype(BF)

    drive([group(g) for g in range(NG_E)])
    start(True)

    @pl.when(step == pl.num_programs(0) - 1)
    def _():
        for late in (False, True):
            for copy in copies(step - 1, 1 - slot, late) + copies(step, slot, late):
                copy.wait()


def zero_first(refs):
    @pl.when(pl.program_id(0) == 0)
    def _():
        for ref in refs:
            ref[...] = jnp.zeros_like(ref)


ACC = [
    ((4, D, S), F32),
    ((3 * D, D), F32),
    ((D + HEAD, D), F32),
    ((FF, 2 * D), F32),
    ((FF + HEAD, D), F32),
]


def finish(acc, out, a_mask=None):
    a_vec, a_wi, a_wo, a_m1, a_m2 = acc

    @pl.when(pl.program_id(0) == pl.num_programs(0) - 1)
    def _():
        out[0:FF, :] = a_m2[0:FF, :] * 0.5
        for j in range(4):
            rows = slice(j * D, (j + 1) * D)
            out[FF + j * D:FF + (j + 1) * D, :] = jnp.transpose(a_m1[rows, 0:D])
            out[SMALL + 6 + j:SMALL + 7 + j, :] = jnp.transpose(a_m1[rows, D:2 * D])[0:1]
            out[SMALL + j:SMALL + j + 1, :] = jnp.sum(jnp.transpose(a_vec[j]), axis=0, keepdims=True)
        for j in range(3):
            rows = slice(j * D, (j + 1) * D)
            out[2 * FF + j * D:2 * FF + (j + 1) * D, :] = jnp.transpose(a_wi[rows, :])
        out[2 * FF + 3 * D:SMALL, :] = a_wo[0:D, :]
        out[SMALL + 4:SMALL + 5, :] = a_wo[D:D + 1, :]
        out[SMALL + 5:SMALL + 6, :] = a_m2[FF:FF + 1, :]
        out[SMALL + 11:PACKED, :] = jnp.zeros((PACKED - SMALL - 11, D), F32)
        out[SMALL + 10:SMALL + 11, :] = jnp.zeros((1, D), F32)
        if a_mask is not None:
            out[SMALL + 10:SMALL + 11, :] = jnp.sum(jnp.transpose(a_mask[...]), axis=0, keepdims=True)


def decode_kernel(inv_order, enc_ref, *rest):
    cots = rest[:(NT * NG_D)]
    seg_ref, vis_ref, mask_row = rest[(NT * NG_D):(NT * NG_D) + 3]
    rest = rest[(NT * NG_D) + 3:]
    raw, rest = rest[:len(RAW)], rest[len(RAW):]
    dec_out, ge_ref, out_ref = rest[:3]
    rest = rest[3:]
    acc, rest = rest[:len(ACC)], rest[len(ACC):]
    a_mask, maskcol, dec_ref, sems = rest[:4]
    rest = rest[4:]
    w = prep_weights(1, raw, rest[:len(PREP)], True)
    scr = rest[len(PREP):]
    step = pl.program_id(0)
    slot = lax.rem(step, 2)

    @pl.when(step == 0)
    def _():
        maskcol[...] = spread_row(mask_row[0:1, :])

    def copies(at, where):
        return [
            pltpu.make_async_copy(dec_ref.at[where, t], dec_out.at[inv_order[(NT * NG_D) * at + t]], sems.at[where, t])
            for t in range((NT * NG_D))
        ]

    @pl.when(step >= 2)
    def _():
        for copy in copies(step - 2, slot):
            copy.wait()

    zero_first(acc + (a_mask,))
    table = list(SAVED) + list(BACK)
    share = sharing([views(table, scr, g) for g in range(NG_D)], TURN_D, lambda g: views(table, scr, g),
                    lambda g: masks(seg_ref, vis_ref, NT * g, True))

    def group(g):
        sv = share["views"][g]
        bias = masks(seg_ref, vis_ref, NT * g, True)
        shown = jnp.concatenate([vis_ref[0, NT * g + t:NT * g + t + 1, :] for t in range(NT)], axis=1) == 1
        x = jnp.where(shown, enc_ref[g].astype(F32), wide(maskcol[...]))
        yield
        out = yield from layer_fwd(x, bias, w, sv, share)
        outb = out.astype(BF)
        for t in range(NT):
            dec_ref[slot, NT * g + t] = jnp.transpose(outb[:, t * S:(t + 1) * S])
        yield
        grad = jnp.concatenate([jnp.transpose(cots[NT * g + t][0]).astype(F32) for t in range(NT)], axis=1)
        yield
        grad = yield from layer_bwd(grad, w, sv, acc, share)
        a_mask[...] += fold(jnp.where(shown, 0.0, grad))
        ge_ref[g] = jnp.where(shown, grad, 0.0).astype(BF)

    drive([group(g) for g in range(NG_D)])
    for copy in copies(step, slot):
        copy.start()

    @pl.when(step == pl.num_programs(0) - 1)
    def _():
        for copy in copies(step - 1, 1 - slot) + copies(step, slot):
            copy.wait()

    finish(acc, out_ref, a_mask)


def back_kernel(core_ref, ge_ref, other_ref, *rest):
    saved = rest[:len(SAVED)]
    rest = rest[len(SAVED):]
    raw, rest = rest[:len(RAW)], rest[len(RAW):]
    tg_ref, keep_ref, send_ref = rest[:3]
    out_ref, rest = rest[3], rest[4:]
    acc, rest = rest[:len(ACC)], rest[len(ACC):]
    w = prep_weights(0, raw, rest[:len(PREP)], False)
    scr = rest[len(PREP):]
    zero_first(acc)
    share = sharing([views(SAVED, saved, g) | views(BACK, scr, g) for g in range(NG_B)], TURN_B, None, None)

    def group(g):
        sv = share["views"][g]
        grad = ge_ref[g].astype(F32)
        yield
        grad = yield from layer_bwd(grad, w, sv, acc, share)
        for t in range(NT):
            tg_ref[NT * g + t] = jnp.transpose(grad[:, t * S:(t + 1) * S])

    drive([group(g) for g in range(NG_B)])
    finish(acc, out_ref)

    @pl.when((pl.program_id(0) == pl.num_programs(0) - 1) & (core_ref[0] == 0))
    def _():
        keep_ref[...] = out_ref[...]
        send_ref[...] = other_ref[...].astype(BF)

    @pl.when((pl.program_id(0) == pl.num_programs(0) - 1) & (core_ref[0] == 1))
    def _():
        keep_ref[...] = other_ref[...]
        send_ref[...] = out_ref[...].astype(BF)


def const_spec(arr):
    return pl.BlockSpec(arr.shape, lambda *_: (0,) * arr.ndim)


def step_spec(shape):
    return pl.BlockSpec(shape, lambda i, *_: (i,) + (0,) * (len(shape) - 1))


PARAMS = pltpu.CompilerParams(dimension_semantics=("arbitrary",), vmem_limit_bytes=60 * 1024 * 1024)
GRADS = [jax.ShapeDtypeStruct((PACKED, D), F32)]


def cost(flops, nbytes):
    return pl.CostEstimate(flops=flops, bytes_accessed=nbytes, transcendentals=0)


def run_encode(x, seg, vis, w):
    tiles = x.shape[0]
    groups, steps = tiles // NT, tiles // (NT * NG_E)
    ops = list(w)
    out_shape = [jax.ShapeDtypeStruct((groups, D, L), BF)]
    out_shape += [jax.ShapeDtypeStruct((groups,) + shape, dt) for shape, dt in SAVED.values()]
    return pl.pallas_call(
        encode_kernel,
        grid=(steps,),
        in_specs=[step_spec(((NT * NG_E), S, D)), step_spec((1, (NT * NG_E), S)), step_spec((1, (NT * NG_E), S))] + [const_spec(o) for o in ops],
        out_specs=[step_spec((NG_E, D, L))] + [pl.BlockSpec(memory_space=pl.ANY)] * len(SAVED),
        out_shape=out_shape,
        scratch_shapes=[pltpu.VMEM((2, NG_E) + shape, dt) for shape, dt in SAVED.values()]
        + [pltpu.SemaphoreType.DMA((2, len(SAVED)))] + prep_scratch(),
        cost_estimate=cost(20 * 10**9, 60 * 10**6),
        compiler_params=PARAMS,
    )(x, seg.reshape(steps, (NT * NG_E), S), vis.reshape(steps, (NT * NG_E), S), *ops)


def run_decode(inv_order, enc, cot, seg, vis, mask_row, w):
    tiles = cot.shape[0]
    groups, steps = tiles // NT, tiles // (NT * NG_D)
    ops = [mask_row] + list(w)
    cot_specs = [pl.BlockSpec((1, S, D), lambda i, o, t=t: (o[(NT * NG_D) * i + t], 0, 0)) for t in range((NT * NG_D))]
    out_shape = [jax.ShapeDtypeStruct((tiles, S, D), BF), jax.ShapeDtypeStruct((groups, D, L), BF)] + GRADS
    return pl.pallas_call(
        decode_kernel,
        grid_spec=pltpu.PrefetchScalarGridSpec(
            num_scalar_prefetch=1,
            grid=(steps,),
            in_specs=[step_spec((NG_D, D, L))] + cot_specs + [step_spec((1, (NT * NG_D), S))] * 2 + [const_spec(o) for o in ops],
            out_specs=[pl.BlockSpec(memory_space=pl.ANY), step_spec((NG_D, D, L))] + [const_spec(o) for o in GRADS],
            scratch_shapes=[pltpu.VMEM(shape, dt) for shape, dt in ACC] + [pltpu.VMEM((D, S), F32)] * 2
            + [pltpu.VMEM((2, (NT * NG_D), S, D), BF), pltpu.SemaphoreType.DMA((2, (NT * NG_D)))]
            + prep_scratch() + scratch_of(SAVED, NG_D) + scratch_of(BACK, NG_D),
        ),
        out_shape=out_shape,
        cost_estimate=cost(40 * 10**9, 10 * 10**6),
        compiler_params=PARAMS,
    )(inv_order, enc, *([cot] * (NT * NG_D)), seg.reshape(steps, (NT * NG_D), S), vis.reshape(steps, (NT * NG_D), S), *ops)


def run_back(core, ge, other, saved, w):
    groups = ge.shape[0]
    steps = groups // NG_B
    ops = list(w)
    packed = jax.ShapeDtypeStruct((PACKED, D), F32)
    out_shape = [jax.ShapeDtypeStruct((groups * NT, S, D), F32), packed, jax.ShapeDtypeStruct((PACKED, D), BF)]
    return pl.pallas_call(
        back_kernel,
        grid_spec=pltpu.PrefetchScalarGridSpec(
            num_scalar_prefetch=1,
            grid=(steps,),
            in_specs=[step_spec((NG_B, D, L)), const_spec(other)] + [step_spec((NG_B,) + v.shape[1:]) for v in saved]
            + [const_spec(o) for o in ops],
            out_specs=[step_spec((NT * NG_B, S, D))] + [const_spec(o) for o in out_shape[1:]],
            scratch_shapes=[pltpu.VMEM((PACKED, D), F32)] + [pltpu.VMEM(shape, dt) for shape, dt in ACC] + prep_scratch()
            + scratch_of(BACK, NG_B),
        ),
        out_shape=out_shape,
        compiler_params=PARAMS,
        cost_estimate=cost(20 * 10**9, 60 * 10**6),
    )(core, ge, other, *saved, *ops)


def unpack_kernel(core_ref, mine, other, g_m2, g_m1, g_wi, g_wo, g_gain, g_shift, g_hid, g_mask):
    core = core_ref[0]

    def write(src, l):
        g_m2[l] = src[0:FF, :].astype(F32)
        for j in range(4):
            g_m1[l, :, j * D:(j + 1) * D] = src[FF + j * D:FF + (j + 1) * D, :].astype(F32)
        for j in range(3):
            g_wi[l, :, j * D:(j + 1) * D] = src[2 * FF + j * D:2 * FF + (j + 1) * D, :].astype(F32)
        g_wo[l] = src[2 * FF + 3 * D:SMALL, :].astype(F32)
        rows = src[SMALL:SMALL + 16, :].astype(F32)
        g_gain[l] = rows[0:2]
        g_shift[l] = rows[2:6]
        for j in range(4):
            g_hid[l:l + 1, j * D:(j + 1) * D] = rows[6 + j:7 + j]
        if l == 1:
            g_mask[...] = rows[10:11]

    @pl.when(core == 0)
    def _():
        write(mine, 0)
        write(other, 1)

    @pl.when(core == 1)
    def _():
        write(other, 0)
        write(mine, 1)


def unpack(core, mine, other):
    shapes = [(2, FF, D), (2, D, FF), (2, D, 3 * D), (2, D, D), (2, 2, D), (2, 4, D), (2, FF), (1, D)]
    return pl.pallas_call(
        unpack_kernel,
        grid_spec=pltpu.PrefetchScalarGridSpec(
            num_scalar_prefetch=1,
            grid=(1,),
            in_specs=[const_spec(mine), const_spec(other)],
            out_specs=[pl.BlockSpec(sh, lambda *_, n=len(sh): (0,) * n) for sh in shapes],
        ),
        out_shape=[jax.ShapeDtypeStruct(sh, F32) for sh in shapes],
        compiler_params=PARAMS,
    )(core.reshape(1).astype(jnp.int32), mine, other)


def partner(i, first, second, n_group):
    dp, x = i // n_group, i % n_group
    y, z, core = dp // 8, dp % 8 // 2, dp % 2
    axis, bits = second if core else first
    if axis == "x":
        x ^= bits
    elif axis == "y":
        y ^= bits
    else:
        z ^= bits
    return (y * 8 + z * 2 + core) * n_group + x


def swap(value, first, second, n_dp, n_group):
    pairs = [(i, partner(i, first, second, n_group)) for i in range(n_dp * n_group)]
    return lax.ppermute(value, ("dp", "group"), pairs)


def swap_cores(value, n_dp):
    return lax.ppermute(value, "dp", [(i, i ^ 1) for i in range(n_dp)])


def reduce_all(core, keep, send, n_dp, n_group):
    place = jnp.where(core == 0, lax.axis_index("group"), lax.axis_index("dp") // 8)
    value = keep + swap_cores(send, n_dp).astype(F32)
    quarter = value.shape[0] // 4
    whole = value
    value = lax.dynamic_slice_in_dim(whole, place * quarter, quarter, axis=0)
    for bits in (1, 2, 3):
        send = lax.dynamic_slice_in_dim(whole, (place ^ bits) * quarter, quarter, axis=0).astype(BF)
        value = value + swap(send, ("x", bits), ("y", bits), n_dp, n_group).astype(F32)
    for first, second in (("y", "z"), ("z", "x")):
        value = lax.reduce_precision(value, 8, 7)
        one, two, three = [swap(value.astype(BF), (first, bits), (second, bits), n_dp, n_group) for bits in (1, 2, 3)]
        value = (value + one.astype(F32)) + (two.astype(F32) + three.astype(F32))
    value = value.astype(BF)
    pieces = [value] + [swap(value, ("x", bits), ("y", bits), n_dp, n_group) for bits in (1, 2, 3)]
    ordered = []
    for j in range(4):
        away = place ^ j
        low = jnp.where(away == 0, pieces[0], pieces[1])
        ordered.append(jnp.where(away < 2, low, jnp.where(away == 2, pieces[2], pieces[3])))
    value = jnp.concatenate(ordered, axis=0)
    return value, swap_cores(value, n_dp)


def on_device(token_tiles, segment_ids, visible_flags, tile_order, mask_token, norm_gains, shift_terms,
              attn_in, attn_out, mlp_in, hidden_shift, mlp_out, cotangent):
    tiles = token_tiles.shape[2]
    full_shape = (1, 1, tiles, S, D)
    order = tile_order.reshape(tiles)
    spots = jnp.arange(tiles, dtype=jnp.int32)
    inv_order = jnp.sum(jnp.where(order[None, :] == spots[:, None], spots[None, :], 0), axis=1).astype(jnp.int32)
    cot = lax.all_to_all(cotangent.reshape(tiles, S, D), "dp", split_axis=0, concat_axis=0, tiled=True)
    w = (norm_gains, shift_terms, hidden_shift, attn_in, attn_out, mlp_in, mlp_out)
    seg, vis = segment_ids.reshape(tiles, S), visible_flags.reshape(tiles, S)
    enc, *saved = run_encode(token_tiles.reshape(tiles, S, D), seg, vis, w)
    dec, ge, packed1 = run_decode(inv_order, enc, cot, seg, vis, mask_token.reshape(1, D), w)
    decoded = lax.all_to_all(dec, "dp", split_axis=0, concat_axis=0, tiled=True)
    core = lax.rem(lax.axis_index("dp"), 2).astype(jnp.int32)
    tg, keep, send = run_back(core.reshape(1), ge, packed1, saved, w)
    n_dp = lax.axis_size("dp")
    if n_dp == 32:
        decoded, send = lax.optimization_barrier((decoded, send))
        mine, other = reduce_all(core, keep, send, n_dp, lax.axis_size("group"))
    else:
        mine, other = keep.astype(BF), send
    g_m2, g_m1, g_wi, g_wo, g_gain, g_shift, g_hid, g_mask = unpack(core, mine, other)
    return (
        decoded.reshape(full_shape),
        tg.reshape(full_shape),
        g_mask.reshape(D),
        g_gain,
        g_shift,
        g_wi,
        g_wo,
        g_m1,
        g_hid,
        g_m2,
    )


def solution(mesh):
    tile5 = P("dp", "group", None, None, None)
    in_specs = (tile5, P("dp", "group", None, None), P("dp", "group", None, None), P("dp", "group", None),
                P(), P(), P(), P(), P(), P(), P(), P(), tile5)
    out_specs = (tile5, tile5) + (P(),) * 8
    return jax.shard_map(on_device, mesh=mesh, in_specs=in_specs, out_specs=out_specs, check_vma=False)
```
